32 devices in a mesh: span: 4 (over z), shard: 8 (over y, x, core).
Axes of the slice: x: 2, y: 2, z: 4, core: 2. Of those that a mesh axis runs over, the one named last changes fastest.
Arguments:
- tokens: bfloat16 [8192, 1152], P(('span', 'shard')), may hold values from -6 to 6
- out_proj: bfloat16 [1152, 1152], replicated, may hold values from -0.1875 to 0.1875
- phi_mean: float32 [1152], replicated, may hold values from -6 to 6
- phi_rotate: bfloat16 [1152, 576], replicated, may hold values from -0.1875 to 0.1875
- destinations: int32 [8192, 1], P(('span', 'shard')), may hold values from 0 to 3; in each aligned block of 256 rows (0 to 255, 256 to 511, ...) at most 96 rows name the same one
- student_hidden: bfloat16 [12288, 1280], P(('span', 'shard')), may hold values from -6 to 6
- adaptor: bfloat16 [1280, 576], replicated, may hold values from -0.15625 to 0.15625
- master: float32 [1280, 576], P('shard'), may hold values from -0.15625 to 0.15625
- moment_one: float32 [1280, 576], P('shard'), may hold values from -4 to 4
- moment_two: float32 [1280, 576], P('shard'), may hold values from 0.01 to 1
Outputs:
- updated_master: float32 [1280, 576], P('shard')
- updated_first: float32 [1280, 576], P('shard')
- updated_second: float32 [1280, 576], P('shard')
The draws below stay inside these ranges and needn't reach their ends.
Inputs may be any that keep to these rules, and one draw needn't show every extreme that they name: `destinations`: at most 96 of the 256 rows of one device name one span; some span gets exactly 96.
All inputs are finite; a program needn't handle non-finite values.
Results may differ from the reference program's by a relative error of at most 0.00064.
Values may be sent and summed in bfloat16 or wider, within the bound.
A program may use at most 64 MiB of HBM per device.

```python
import math
import jax
import jax.numpy as jnp
import numpy as np
from jax import lax

DT = 1152
DW = 576
H = 1280
ROWS_DEV = 256
ADAM_STEP = 1000
CAP = 96
SLOTS = 384
TEACH_ROWS = 8192
STUD_SLOTS = 12288
N_SPAN = 4
N_SHARD = 8


def spiked(values, own_key, source, target, blocks, factor):
    owner, partner = [(jnp.arange(values.shape[dim]) // (values.shape[dim] // blocks)).reshape([-1 if axis == dim else 1 for axis in range(values.ndim)]) for dim in (source, target)]
    chosen = jax.random.permutation(own_key, blocks)[partner]
    strong = (owner == chosen) | (owner == (partner + blocks // 2) % blocks)
    return jnp.where(strong, factor * values, values)


def level_of(own_key, extent, cuts, smallest, high):
    level = 1.0
    for axis_at, blocks in cuts:
        steps = jax.random.uniform(jax.random.fold_in(jax.random.fold_in(own_key, 6), axis_at), (blocks,), jnp.float32, smallest / len(cuts), high / len(cuts))
        level = level * jnp.repeat(jnp.exp(steps), extent[axis_at] // blocks).reshape((-1,) + (1,) * (len(extent) - 1 - axis_at))
    return level


def routed_block(stream_key, own, number, rows, count, top, limit, skew):
    sequence = jax.random.permutation(stream_key, count)
    packed, usual = shares(count, rows * top, limit, skew, True), shares(count, rows * top, limit, skew, False)
    places = jnp.arange(count)

    def named(tallies, offset_by):
        used = int((tallies > 0).sum())
        fixed = max(1, used // 4)
        passed = fixed + (places - fixed + offset_by * (used - fixed)) % max(1, count - fixed)
        return jnp.zeros((count,), jnp.int32).at[sequence[jnp.where(places < fixed, places, passed)]].set(jnp.asarray(tallies, jnp.int32))

    tallies = jnp.where(number % 4 == 0, named(packed, number // 4), named(usual, number - number // 4 - 1))
    mixed = jax.random.permutation(jax.random.fold_in(own, 3), count)
    donor, sink = mixed[0:count // 2 * 2:2], mixed[1:count // 2 * 2:2]
    margin = jnp.minimum(tallies[donor] - 1, limit - tallies[sink]) // 2
    margin = jnp.where((donor == sequence[0]) | (sink == sequence[0]) | (tallies[sink] == 0), 0, jnp.maximum(margin, 0))
    passed = jax.random.randint(jax.random.fold_in(own, 4), (count // 2,), 0, 1 << 20) % (margin + 1)
    tallies = tallies.at[donor].add(-passed).at[sink].add(passed)
    labels = jnp.searchsorted(jnp.cumsum(tallies), jnp.arange(rows * top), side="right").astype(jnp.int32)
    listing = labels.reshape(top, rows).T
    listing = listing[jax.random.permutation(jax.random.fold_in(own, 1), rows)]
    offset_by = jax.random.randint(jax.random.fold_in(own, 2), (rows, 1), 0, top)
    return jnp.take_along_axis(listing, (jnp.arange(top)[None, :] + offset_by) % top, axis=1)


def shares(amount, total, limit, skew, full):
    loads = [(1 << 20) // math.isqrt(grade ** skew) + 1 for grade in range(1, amount + 1)]
    largest = limit if full else min(limit, max(-(-total // amount), total * loads[0] // sum(loads)))
    least = 1 if total - largest >= amount - 1 else 0
    given, spare = [largest] + [least] * (amount - 1), total - largest - least * (amount - 1)
    while spare > 0:
        movable = [i for i in range(1, amount) if given[i] < largest] or [i for i in range(1, amount) if given[i] < limit]
        pool, remaining = sum([loads[i] for i in movable]), spare
        for i in movable:
            more = min(limit - given[i], max(1, remaining * loads[i] // pool), spare)
            given[i] = given[i] + more
            spare = spare - more
    return np.array(given)


def normal_values(key, extent, width, most, pieces=(), kind=jnp.bfloat16):
    entries = jax.random.normal(key, extent, jnp.float32) * width
    if len(pieces) > 0:
        entries = level_of(key, extent, pieces, -0.22, 0.18) * entries
    return jnp.clip(entries, min=-most, max=most).astype(kind)


def heavy_noise(rng, extent, spread, bound, split, heavy, kind=jnp.bfloat16):
    values = spread * jax.random.normal(rng, extent, jnp.float32)
    if split:
        values = values * level_of(rng, extent, split, -0.22, 0.18)
    return jnp.clip(spiked(values, jax.random.fold_in(rng, 3), *heavy), -bound, bound).astype(kind)


def setup_inputs(seed: int = 0) -> dict:
    key_of = jax.random.split(jax.random.key(seed), 11)
    tokens = normal_values(key_of[0], (TEACH_ROWS, DT), 1.0, 6.0, ((0, 32),))
    out_proj = normal_values(key_of[1], (DT, DT), DT ** -0.5, 0.1875)
    phi_mean = normal_values(key_of[2], (DT,), 1.0, 6.0, (), jnp.float32)
    phi_rotate = normal_values(key_of[3], (DT, DW), DT ** -0.5, 0.1875)
    destinations_keys = jax.random.split(jax.random.fold_in(key_of[4], 1), TEACH_ROWS // ROWS_DEV)
    destinations_turns = jax.random.permutation(jax.random.fold_in(key_of[4], 3), TEACH_ROWS // ROWS_DEV)
    destinations = jax.vmap(lambda own, number: routed_block(jax.random.fold_in(key_of[4], 2), own, number, ROWS_DEV, N_SPAN, 1, CAP, 2))(destinations_keys, destinations_turns).reshape((TEACH_ROWS, 1))
    student_hidden = heavy_noise(key_of[5], (STUD_SLOTS, H), 1.0, 6.0, ((0, 32),), (0, 1, 32, 2.75))
    adaptor = normal_values(key_of[6], (H, DW), H ** -0.5, 0.15625)
    master = normal_values(key_of[7], (H, DW), H ** -0.5, 0.15625, ((0, 8),), jnp.float32)
    moment_one = normal_values(key_of[8], (H, DW), 0.3, 4.0, ((0, 8),), jnp.float32)
    moment_two = jnp.clip(jnp.exp(math.log(1.0) - 4.6051702 * jax.random.uniform(key_of[9], (H, DW), jnp.float32) ** level_of(key_of[9], (H, DW), ((0, 8),), -0.2, 0.2)), 0.01, 1.0)
    return dict(tokens=tokens, out_proj=out_proj, phi_mean=phi_mean, phi_rotate=phi_rotate, destinations=destinations, student_hidden=student_hidden, adaptor=adaptor, master=master, moment_one=moment_one, moment_two=moment_two)


beta_first = 0.9
beta_second = 0.999
adam_epsilon = 1e-08
decay_rate = 0.05
learn_rate = 0.001

def reference(tokens, out_proj, phi_mean, phi_rotate, destinations, student_hidden, adaptor, master, moment_one, moment_two):
    span_count = N_SPAN
    shard_count = N_SHARD
    target_span = destinations[:, 0].reshape(span_count, shard_count, ROWS_DEV)
    span_ids = jnp.arange(span_count, dtype=jnp.int32)
    one_hot = (target_span[..., None] == span_ids).astype(jnp.int32)
    slot_rank = lax.optimization_barrier(jnp.sum((jnp.cumsum(one_hot, axis=2) - one_hot) * one_hot, axis=3))
    source = span_ids[:, None, None]
    shard_ids = jnp.arange(shard_count, dtype=jnp.int32)[None, :, None]
    placement_ids = ((target_span * shard_count + shard_ids) * SLOTS + source * CAP + slot_rank).astype(jnp.int32)
    token_blocks = tokens.reshape(span_count, shard_count * ROWS_DEV, DT)
    place_blocks = placement_ids.reshape(span_count, shard_count * ROWS_DEV)

    def one_span(running, paired):
        block_rows, block_place = paired
        projected = (jnp.dot(block_rows, out_proj, preferred_element_type=jnp.float32) - phi_mean).astype(jnp.bfloat16)
        target = jnp.dot(projected, phi_rotate, preferred_element_type=jnp.float32).astype(jnp.bfloat16)
        hidden = student_hidden[block_place]
        activated = jax.nn.gelu(hidden.astype(jnp.float32), approximate=False).astype(jnp.bfloat16)
        predicted = jnp.dot(activated, adaptor, preferred_element_type=jnp.float32)
        scaled_error = ((predicted - target.astype(jnp.float32)) / DW).astype(jnp.bfloat16)
        return (running + jnp.dot(activated.T, scaled_error, preferred_element_type=jnp.float32), None)
    gradient, unused = lax.scan(one_span, jnp.zeros((H, DW), jnp.float32), (token_blocks, place_blocks))
    first_new = beta_first * moment_one + (1.0 - beta_first) * gradient
    second_new = beta_second * moment_two + (1.0 - beta_second) * gradient * gradient
    bias_first = 1.0 - beta_first ** ADAM_STEP
    bias_second = 1.0 - beta_second ** ADAM_STEP
    update_dir = first_new / bias_first / (jnp.sqrt(second_new / bias_second) + adam_epsilon) + decay_rate * master
    return (master - learn_rate * update_dir, first_new, second_new)
```

```python
import functools

import jax
import jax.numpy as jnp
from jax import lax
from jax.experimental import pallas as pl
from jax.experimental.pallas import tpu as pltpu
from jax.sharding import PartitionSpec as P

ADAM_STEP = 1000


beta_first = 0.9
beta_second = 0.999
adam_epsilon = 1e-08
decay_rate = 0.05
learn_rate = 0.001

EMPTY = 2.0**100
EMPTY_TEST = 2.0**90
MESH = pl.DeviceIdType.MESH


def adam_update(gradient, master, moment_one, moment_two):
    first_new = beta_first * moment_one + (1.0 - beta_first) * gradient
    second_new = beta_second * moment_two + (1.0 - beta_second) * gradient * gradient
    bias_first = 1.0 - beta_first**ADAM_STEP
    bias_second = 1.0 - beta_second**ADAM_STEP
    update_dir = (
        first_new / bias_first / (jnp.sqrt(second_new / bias_second) + adam_epsilon)
        + decay_rate * master
    )
    return (master - learn_rate * update_dir, first_new, second_new)


def route_slots(destinations, span_count, capacity):
    target_span = destinations[:, 0]
    span_ids = jnp.arange(span_count, dtype=jnp.int32)
    one_hot = (target_span[:, None] == span_ids[None, :]).astype(jnp.int32)
    before = jnp.cumsum(one_hot, axis=0) - one_hot
    slot_rank = jnp.sum(before * one_hot, axis=1)
    return target_span * capacity + slot_rank


def general_body(
    tokens,
    out_proj,
    phi_mean,
    phi_rotate,
    destinations,
    student_hidden,
    adaptor,
    master,
    moment_one,
    moment_two,
):
    span_count = lax.axis_size("span")
    slots = student_hidden.shape[0]
    capacity = slots // span_count
    features = adaptor.shape[1]
    projected = (jnp.dot(tokens, out_proj, preferred_element_type=jnp.float32) - phi_mean).astype(
        jnp.bfloat16
    )
    target = jnp.dot(projected, phi_rotate, preferred_element_type=jnp.float32).astype(jnp.bfloat16)
    slot_ids = route_slots(destinations, span_count, capacity)
    placed = jnp.full((slots, features), EMPTY, jnp.bfloat16).at[slot_ids].set(target)
    arrived = lax.all_to_all(
        placed.reshape(span_count, capacity, features), "span", split_axis=0, concat_axis=0, tiled=True
    ).reshape(slots, features)
    activated = jax.nn.gelu(student_hidden.astype(jnp.float32), approximate=False).astype(jnp.bfloat16)
    predicted = jnp.dot(activated, adaptor, preferred_element_type=jnp.float32)
    wanted = arrived.astype(jnp.float32)
    scaled_error = jnp.where(wanted > EMPTY_TEST, 0.0, (predicted - wanted) / features).astype(
        jnp.bfloat16
    )
    contract = (((0,), (0,)), ((), ()))
    partial_sum = lax.psum_scatter(
        lax.dot_general(activated, scaled_error, contract, preferred_element_type=jnp.float32),
        "shard",
        scatter_dimension=0,
        tiled=True,
    )
    return adam_update(lax.psum(partial_sum, "span"), master, moment_one, moment_two)


SPANS = 4
SHARDS = 8


def chunks_of(features):
    first = features // 2 // 128 * 128
    return ((0, first), (first, features))


def dot(a, b):
    return jnp.dot(a, b, preferred_element_type=jnp.float32)


def step_kernel(
    chunks,
    tokens_hbm,
    proj_hbm,
    mean_hbm,
    rotate_hbm,
    dest_hbm,
    hidden_hbm,
    adaptor_hbm,
    master_hbm,
    one_hbm,
    two_hbm,
    out_master,
    out_first,
    out_second,
    tokens,
    proj,
    mean,
    rotate,
    dest,
    hidden,
    adaptor,
    master,
    one,
    two,
    act,
    act_t,
    pred,
    *rest,
):
    per_chunk, (load_sem, a2a_send, a2a_recv, core_sem, s2_sem, s3_sem, z_send, z_recv) = (
        rest[:-8],
        rest[-8:],
    )
    count = len(per_chunk) // len(chunks)
    buf = [per_chunk[c * count : (c + 1) * count] for c in range(len(chunks))]

    span = lax.axis_index("span")
    me = lax.axis_index("shard")
    core = lax.rem(me, 2)
    my_x = lax.rem(me // 2, 2)
    my_y = me // 4
    core_mate = me + 1 - 2 * core
    x_mate = me + 2 - 4 * my_x
    y_mate = me + 4 - 8 * my_y

    slots, width = hidden.shape
    rows = tokens.shape[0]
    features = adaptor.shape[1]
    cap = slots // SPANS
    block = width // SHARDS
    half = block // 2

    pairs = (
        (tokens_hbm, tokens),
        (proj_hbm, proj),
        (mean_hbm, mean),
        (dest_hbm, dest),
        (rotate_hbm, rotate),
        (hidden_hbm, hidden),
        (adaptor_hbm, adaptor),
        (master_hbm, master),
        (one_hbm, one),
        (two_hbm, two),
    )
    loads = [pltpu.make_async_copy(s, d, load_sem.at[i]) for i, (s, d) in enumerate(pairs)]
    for load in loads:
        load.start()

    barrier = pltpu.get_barrier_semaphore()
    for step in range(1, SPANS):
        pl.semaphore_signal(
            barrier, inc=1, device_id=(lax.rem(span + step, SPANS), me), device_id_type=MESH
        )
    for mate in (core_mate, x_mate, y_mate):
        pl.semaphore_signal(barrier, inc=1, device_id=(span, mate), device_id_type=MESH)

    loads[3].wait()
    wanted = dest[...]
    span_ids = lax.broadcasted_iota(jnp.int32, (16, rows), 0)
    one_hot = jnp.where(span_ids == wanted, 1.0, 0.0)
    earlier = jnp.where(
        lax.broadcasted_iota(jnp.int32, (rows, rows), 0)
        < lax.broadcasted_iota(jnp.int32, (rows, rows), 1),
        1.0,
        0.0,
    ).astype(jnp.bfloat16)
    before = dot(one_hot.astype(jnp.bfloat16), earlier)
    rank = jnp.sum(before * one_hot, axis=0, keepdims=True).astype(jnp.int32)
    slot = wanted * cap + rank
    place = jnp.where(lax.broadcasted_iota(jnp.int32, (slots, rows), 0) == slot, 1.0, 0.0)
    empty = (1.0 - jnp.sum(place, axis=1, keepdims=True)) * EMPTY
    place = place.astype(jnp.bfloat16)

    for i in (0, 1, 2):
        loads[i].wait()
    projected = (dot(tokens[...], proj[...]) - mean[...]).astype(jnp.bfloat16)
    loads[4].wait()
    pl.semaphore_wait(barrier, SPANS - 1 + 3)

    a2a = []
    for c, (lo, hi) in enumerate(chunks):
        t_send, t_recv = buf[c][0], buf[c][1]
        target = dot(projected, rotate[:, lo:hi]).astype(jnp.bfloat16)
        t_send[...] = (dot(place, target) + empty).astype(jnp.bfloat16)
        for step in (2, 3, 1):
            other = lax.rem(span + step, SPANS)
            copy = pltpu.make_async_remote_copy(
                src_ref=t_send.at[pl.ds(pl.multiple_of(other * cap, 16), cap)],
                dst_ref=t_recv.at[pl.ds(pl.multiple_of(span * cap, 16), cap)],
                send_sem=a2a_send.at[c, step - 1],
                recv_sem=a2a_recv.at[c, step - 1],
                device_id=(other, me),
                device_id_type=MESH,
            )
            copy.start()
            a2a.append(copy)
        mine = pl.ds(pl.multiple_of(span * cap, 16), cap)
        t_recv[mine, :] = t_send[mine, :]

    loads[5].wait()
    for j in range(0, width, 128):
        x = hidden[:, j : j + 128].astype(jnp.float32)
        a = (0.5 * x * (1.0 + lax.erf(x * (0.5**0.5)))).astype(jnp.bfloat16)
        act[:, j : j + 128] = a
        act_t[j : j + 128, :] = a.T
    loads[6].wait()
    pred[...] = dot(act[...], adaptor[...])

    sends = []

    def send(src, dst, send_sem, recv_sem, device):
        copy = pltpu.make_async_remote_copy(
            src_ref=src,
            dst_ref=dst,
            send_sem=send_sem,
            recv_sem=recv_sem,
            device_id=device,
            device_id_type=MESH,
        )
        copy.start()
        return copy

    core_copies = {}
    s2_copies = {}
    s3_copies = {}

    def gradient_block(index, error):
        start = pl.multiple_of(index * block, 16)
        return dot(act_t[pl.ds(start, block), :], error)

    def form(c):
        lo, hi = chunks[c]
        t_recv, core_out, core_in, total = buf[c][1], buf[c][2], buf[c][3], buf[c][4]
        for copy in a2a[3 * c : 3 * c + 3]:
            copy.wait_recv()
        t = t_recv[...].astype(jnp.float32)
        error = jnp.where(t > EMPTY_TEST, 0.0, (pred[:, lo:hi] - t) * (1.0 / features)).astype(
            jnp.bfloat16
        )
        for j in range(4):
            core_out[j] = gradient_block(2 * j + 1 - core, error).astype(jnp.bfloat16)
        core_copies[c] = send(
            core_out, core_in, core_sem.at[c, 0], core_sem.at[c, 1], (span, core_mate)
        )
        for j in range(4):
            total[j] = gradient_block(2 * j + core, error)

    def first_axis(c):
        core_in, total = buf[c][3], buf[c][4]
        core_copies[c].wait_recv()
        for h in range(2):
            s2_out, s2_in, kept = buf[c][5 + h], buf[c][7 + h], buf[c][9 + h]
            part = pl.ds(h * half, half)
            for j in range(2):
                away = 2 * j + 1 - my_x if h == 0 else 2 * (1 - my_y) + j
                s2_out[j] = (total[away, part, :] + core_in[away, part, :]).astype(jnp.bfloat16)
            s2_copies[c, h] = send(
                s2_out,
                s2_in,
                s2_sem.at[c, h, 0],
                s2_sem.at[c, h, 1],
                (span, x_mate if h == 0 else y_mate),
            )
            for j in range(2):
                here = 2 * j + my_x if h == 0 else 2 * my_y + j
                kept[j] = total[here, part, :] + core_in[here, part, :]

    def second_axis(c):
        for h in range(2):
            s2_in, kept, s3_out, s3_in = buf[c][7 + h], buf[c][9 + h], buf[c][11 + h], buf[c][13 + h]
            s2_copies[c, h].wait_recv()
            bit = my_y if h == 0 else my_x
            s3_out[...] = kept[1 - bit] + s2_in[1 - bit]
            s3_copies[c, h] = send(
                s3_out,
                s3_in,
                s3_sem.at[c, h, 0],
                s3_sem.at[c, h, 1],
                (span, y_mate if h == 0 else x_mate),
            )

    inner = jnp.logical_and(span >= 1, span <= 2)
    outer = jnp.logical_not(inner)
    near = jnp.where(span < 2, 1 - span, 5 - span)

    def z_copy(c, h, kind):
        z_out, z_one, z_two, z_end = buf[c][15 + h], buf[c][17 + h], buf[c][19 + h], buf[c][21 + h]
        src, dst, other = {
            "in": (z_out, z_one, near),
            "across": (z_out, z_two, 3 - span),
            "back": (z_end, z_end, near),
        }[kind]
        slot_of = {"in": 0, "across": 1, "back": 2}[kind]
        return pltpu.make_async_remote_copy(
            src_ref=src,
            dst_ref=dst,
            send_sem=z_send.at[c, h, slot_of],
            recv_sem=z_recv.at[c, h, slot_of],
            device_id=(other, me),
            device_id_type=MESH,
        )

    def chain_start(c):
        for h in range(2):
            s2_in, kept, s3_in = buf[c][7 + h], buf[c][9 + h], buf[c][13 + h]
            z_out, z_one = buf[c][15 + h], buf[c][17 + h]
            s3_copies[c, h].wait_recv()
            bit = my_y if h == 0 else my_x
            own = kept[bit] + s2_in[bit] + s3_in[...]

            @pl.when(outer)
            def _():
                z_out[...] = own
                z_copy(c, h, "in").start()

            @pl.when(inner)
            def _():
                z_copy(c, h, "in").wait_recv()
                z_out[...] = own + z_one[...]
                z_copy(c, h, "across").start()

    def chain_middle(c):
        for h in range(2):
            z_out, z_two, z_end = buf[c][15 + h], buf[c][19 + h], buf[c][21 + h]

            @pl.when(inner)
            def _():
                z_copy(c, h, "across").wait_recv()
                z_end[...] = z_out[...] + z_two[...]
                z_copy(c, h, "back").start()

    def finish(c):
        lo, hi = chunks[c]
        for h in range(2):
            z_end = buf[c][21 + h]

            @pl.when(outer)
            def _():
                z_copy(c, h, "back").wait_recv()

            part = pl.ds(h * half, half)
            new = adam_update(
                z_end[...], master[part, lo:hi], one[part, lo:hi], two[part, lo:hi]
            )
            out_master[part, lo:hi] = new[0]
            out_first[part, lo:hi] = new[1]
            out_second[part, lo:hi] = new[2]

    form(0)
    first_axis(0)
    second_axis(0)
    chain_start(0)
    form(1)
    first_axis(1)
    chain_middle(0)
    second_axis(1)
    for i in (7, 8, 9):
        loads[i].wait()
    chain_start(1)
    finish(0)
    chain_middle(1)
    finish(1)

    for copy in a2a:
        copy.wait_send()
    for c in range(len(chunks)):
        core_copies[c].wait_send()
        for h in range(2):
            s2_copies[c, h].wait_send()
            s3_copies[c, h].wait_send()

            @pl.when(outer)
            def _():
                z_copy(c, h, "in").wait_send()

            @pl.when(inner)
            def _():
                z_copy(c, h, "across").wait_send()
                z_copy(c, h, "back").wait_send()


def kernel_body(
    tokens,
    out_proj,
    phi_mean,
    phi_rotate,
    destinations,
    student_hidden,
    adaptor,
    master,
    moment_one,
    moment_two,
):
    rows = tokens.shape[0]
    slots, width = student_hidden.shape
    features = adaptor.shape[1]
    block = width // SHARDS
    half = block // 2
    chunks = chunks_of(features)
    bf16, f32 = jnp.bfloat16, jnp.float32
    mean = phi_mean.reshape(1, -1)
    dest = destinations.reshape(1, rows)
    inputs = (
        tokens,
        out_proj,
        mean,
        phi_rotate,
        dest,
        student_hidden,
        adaptor,
        master,
        moment_one,
        moment_two,
    )
    scratch = [pltpu.VMEM(a.shape, a.dtype) for a in inputs]
    scratch += [
        pltpu.VMEM((slots, width), bf16),
        pltpu.VMEM((width, slots), bf16),
        pltpu.VMEM((slots, features), f32),
    ]
    for lo, hi in chunks:
        wide = hi - lo
        scratch += [pltpu.VMEM((slots, wide), bf16)] * 2
        scratch += [pltpu.VMEM((4, block, wide), bf16)] * 2
        scratch += [pltpu.VMEM((4, block, wide), f32)]
        scratch += [pltpu.VMEM((2, half, wide), bf16)] * 4
        scratch += [pltpu.VMEM((2, half, wide), f32)] * 2
        scratch += [pltpu.VMEM((half, wide), f32)] * 12
    n = len(chunks)
    dma = pltpu.SemaphoreType.DMA
    scratch += [
        dma((len(inputs),)),
        dma((n, SPANS - 1)),
        dma((n, SPANS - 1)),
        dma((n, 2)),
        dma((n, 2, 2)),
        dma((n, 2, 2)),
        dma((n, 2, 3)),
        dma((n, 2, 3)),
    ]
    flops = 2 * (rows * tokens.shape[1] * (tokens.shape[1] + features) + 2 * slots * width * features)
    return pl.pallas_call(
        functools.partial(step_kernel, chunks),
        out_shape=[jax.ShapeDtypeStruct(master.shape, f32)] * 3,
        in_specs=[pl.BlockSpec(memory_space=pl.ANY)] * len(inputs),
        out_specs=[pl.BlockSpec(memory_space=pltpu.VMEM)] * 3,
        scratch_shapes=scratch,
        compiler_params=pltpu.CompilerParams(
            collective_id=0, has_side_effects=True, vmem_limit_bytes=48 * 2**20
        ),
        cost_estimate=pl.CostEstimate(
            flops=flops, bytes_accessed=10 * 2**20, transcendentals=slots * width
        ),
    )(*inputs)


def solution(mesh):
    in_specs = (
        P(("span", "shard"), None),
        P(),
        P(),
        P(),
        P(("span", "shard"), None),
        P(("span", "shard"), None),
        P(),
        P("shard", None),
        P("shard", None),
        P("shard", None),
    )
    out_specs = (P("shard", None), P("shard", None), P("shard", None))
    tuned = mesh.shape["span"] == SPANS and mesh.shape["shard"] == SHARDS
    body = kernel_body if tuned else general_body
    return jax.shard_map(body, mesh=mesh, in_specs=in_specs, out_specs=out_specs, check_vma=False)
```

```python
import functools

import jax
import jax.numpy as jnp
from jax import lax
from jax.experimental import pallas as pl
from jax.experimental.pallas import tpu as pltpu
from jax.sharding import PartitionSpec as P

ADAM_STEP = 1000


beta_first = 0.9
beta_second = 0.999
adam_epsilon = 1e-08
decay_rate = 0.05
learn_rate = 0.001

EMPTY = 2.0**100
EMPTY_TEST = 2.0**90
MESH = pl.DeviceIdType.MESH


def adam_update(gradient, master, moment_one, moment_two):
    first_new = beta_first * moment_one + (1.0 - beta_first) * gradient
    second_new = beta_second * moment_two + (1.0 - beta_second) * gradient * gradient
    bias_first = 1.0 - beta_first**ADAM_STEP
    bias_second = 1.0 - beta_second**ADAM_STEP
    update_dir = (
        first_new / bias_first / (jnp.sqrt(second_new / bias_second) + adam_epsilon)
        + decay_rate * master
    )
    return (master - learn_rate * update_dir, first_new, second_new)


def route_slots(destinations, span_count, capacity):
    target_span = destinations[:, 0]
    span_ids = jnp.arange(span_count, dtype=jnp.int32)
    one_hot = (target_span[:, None] == span_ids[None, :]).astype(jnp.int32)
    before = jnp.cumsum(one_hot, axis=0) - one_hot
    slot_rank = jnp.sum(before * one_hot, axis=1)
    return target_span * capacity + slot_rank


def general_body(
    tokens,
    out_proj,
    phi_mean,
    phi_rotate,
    destinations,
    student_hidden,
    adaptor,
    master,
    moment_one,
    moment_two,
):
    span_count = lax.axis_size("span")
    slots = student_hidden.shape[0]
    capacity = slots // span_count
    features = adaptor.shape[1]
    projected = (jnp.dot(tokens, out_proj, preferred_element_type=jnp.float32) - phi_mean).astype(
        jnp.bfloat16
    )
    target = jnp.dot(projected, phi_rotate, preferred_element_type=jnp.float32).astype(jnp.bfloat16)
    slot_ids = route_slots(destinations, span_count, capacity)
    placed = jnp.full((slots, features), EMPTY, jnp.bfloat16).at[slot_ids].set(target)
    arrived = lax.all_to_all(
        placed.reshape(span_count, capacity, features), "span", split_axis=0, concat_axis=0, tiled=True
    ).reshape(slots, features)
    activated = jax.nn.gelu(student_hidden.astype(jnp.float32), approximate=False).astype(jnp.bfloat16)
    predicted = jnp.dot(activated, adaptor, preferred_element_type=jnp.float32)
    wanted = arrived.astype(jnp.float32)
    scaled_error = jnp.where(wanted > EMPTY_TEST, 0.0, (predicted - wanted) / features).astype(
        jnp.bfloat16
    )
    contract = (((0,), (0,)), ((), ()))
    partial_sum = lax.psum_scatter(
        lax.dot_general(activated, scaled_error, contract, preferred_element_type=jnp.float32),
        "shard",
        scatter_dimension=0,
        tiled=True,
    )
    return adam_update(lax.psum(partial_sum, "span"), master, moment_one, moment_two)


SPANS = 4
SHARDS = 8


def chunks_of(features):
    last = features // 128 * 128
    first = last // 256 * 128
    return ((0, first), (first, last), (last, features))


def dot(a, b):
    return jnp.dot(a, b, preferred_element_type=jnp.float32)


def dot_t(a, b):
    return lax.dot_general(a, b, (((1,), (1,)), ((), ())), preferred_element_type=jnp.float32)


def step_kernel(
    chunks,
    tokens_hbm,
    proj_hbm,
    mean_hbm,
    rotate_hbm,
    dest_hbm,
    hidden_hbm,
    adaptor_hbm,
    master_hbm,
    one_hbm,
    two_hbm,
    out_master,
    out_first,
    out_second,
    tokens,
    proj,
    mean,
    rotate,
    dest,
    hidden,
    adaptor,
    master,
    one,
    two,
    act,
    act_t,
    pred,
    *rest,
):
    per_chunk, (load_sem, a2a_send, a2a_recv, core_sem, s2_sem, s3_sem, z_send, z_recv) = (
        rest[:-8],
        rest[-8:],
    )
    count = len(per_chunk) // len(chunks)
    buf = [per_chunk[c * count : (c + 1) * count] for c in range(len(chunks))]

    span = lax.axis_index("span")
    me = lax.axis_index("shard")
    core = lax.rem(me, 2)
    my_x = lax.rem(me // 2, 2)
    my_y = me // 4
    core_mate = me + 1 - 2 * core
    x_mate = me + 2 - 4 * my_x
    y_mate = me + 4 - 8 * my_y

    slots, width = hidden.shape
    rows = tokens.shape[0]
    features = adaptor.shape[0]
    cap = slots // SPANS
    block = width // SHARDS
    half = block // 2

    pairs = (
        (tokens_hbm, tokens),
        (proj_hbm, proj),
        (mean_hbm, mean),
        (dest_hbm, dest),
        (rotate_hbm, rotate),
        (hidden_hbm, hidden),
        (adaptor_hbm, adaptor),
        (master_hbm, master),
        (one_hbm, one),
        (two_hbm, two),
    )
    loads = [pltpu.make_async_copy(s, d, load_sem.at[i]) for i, (s, d) in enumerate(pairs)]
    for load in loads:
        load.start()

    barrier = pltpu.get_barrier_semaphore()
    for step in range(1, SPANS):
        pl.semaphore_signal(
            barrier, inc=1, device_id=(lax.rem(span + step, SPANS), me), device_id_type=MESH
        )
    for mate in (core_mate, x_mate, y_mate):
        pl.semaphore_signal(barrier, inc=1, device_id=(span, mate), device_id_type=MESH)

    loads[3].wait()
    wanted = dest[...]
    span_ids = lax.broadcasted_iota(jnp.int32, (16, rows), 0)
    one_hot = jnp.where(span_ids == wanted, 1.0, 0.0)
    earlier = jnp.where(
        lax.broadcasted_iota(jnp.int32, (rows, rows), 0)
        < lax.broadcasted_iota(jnp.int32, (rows, rows), 1),
        1.0,
        0.0,
    ).astype(jnp.bfloat16)
    before = dot(one_hot.astype(jnp.bfloat16), earlier)
    rank = jnp.sum(before * one_hot, axis=0, keepdims=True).astype(jnp.int32)
    slot = wanted * cap + rank
    place = jnp.where(lax.broadcasted_iota(jnp.int32, (slots, rows), 0) == slot, 1.0, 0.0)
    empty = (1.0 - jnp.sum(place, axis=1, keepdims=True)) * EMPTY
    place = place.astype(jnp.bfloat16)

    for i in (0, 1, 2):
        loads[i].wait()
    projected = (dot(tokens[...], proj[...]) - mean[...].reshape(1, -1)).astype(jnp.bfloat16)
    loads[4].wait()
    pl.semaphore_wait(barrier, SPANS - 1 + 3)

    a2a = []
    for c, (lo, hi) in enumerate(chunks):
        t_send, t_recv = buf[c][0], buf[c][1]
        target = dot_t(projected, rotate[lo:hi, :]).astype(jnp.bfloat16)
        t_send[...] = (dot(place, target) + empty).astype(jnp.bfloat16)
        for step in (2, 3, 1):
            other = lax.rem(span + step, SPANS)
            copy = pltpu.make_async_remote_copy(
                src_ref=t_send.at[pl.ds(pl.multiple_of(other * cap, 16), cap)],
                dst_ref=t_recv.at[pl.ds(pl.multiple_of(span * cap, 16), cap)],
                send_sem=a2a_send.at[c, step - 1],
                recv_sem=a2a_recv.at[c, step - 1],
                device_id=(other, me),
                device_id_type=MESH,
            )
            copy.start()
            a2a.append(copy)
        mine = pl.ds(pl.multiple_of(span * cap, 16), cap)
        t_recv[mine, :] = t_send[mine, :]

    loads[5].wait()
    for j in range(0, width, 128):
        x = hidden[:, j : j + 128].astype(jnp.float32)
        a = (0.5 * x * (1.0 + lax.erf(x * (0.5**0.5)))).astype(jnp.bfloat16)
        act[:, j : j + 128] = a
        act_t[j : j + 128, :] = a.T
    loads[6].wait()
    pred[...] = dot_t(act[...], adaptor[...])

    sends = []

    def send(src, dst, send_sem, recv_sem, device):
        copy = pltpu.make_async_remote_copy(
            src_ref=src,
            dst_ref=dst,
            send_sem=send_sem,
            recv_sem=recv_sem,
            device_id=device,
            device_id_type=MESH,
        )
        copy.start()
        return copy

    core_copies = {}
    s2_copies = {}
    s3_copies = {}

    def gradient_block(index, error):
        start = pl.multiple_of(index * block, 16)
        return dot(act_t[pl.ds(start, block), :], error)

    def form(c):
        lo, hi = chunks[c]
        t_recv, core_out, core_in, total = buf[c][1], buf[c][2], buf[c][3], buf[c][4]
        for copy in a2a[3 * c : 3 * c + 3]:
            copy.wait_recv()
        t = t_recv[...].astype(jnp.float32)
        error = jnp.where(t > EMPTY_TEST, 0.0, (pred[:, lo:hi] - t) * (1.0 / features)).astype(
            jnp.bfloat16
        )
        for j in range(4):
            core_out[j] = gradient_block(2 * j + 1 - core, error).astype(jnp.bfloat16)
        core_copies[c] = send(
            core_out, core_in, core_sem.at[c, 0], core_sem.at[c, 1], (span, core_mate)
        )
        for j in range(4):
            total[j] = gradient_block(2 * j + core, error)

    def first_axis(c):
        core_in, total = buf[c][3], buf[c][4]
        core_copies[c].wait_recv()
        for h in range(2):
            s2_out, s2_in, kept = buf[c][5 + h], buf[c][7 + h], buf[c][9 + h]
            part = pl.ds(h * half, half)
            for j in range(2):
                away = 2 * j + 1 - my_x if h == 0 else 2 * (1 - my_y) + j
                s2_out[j] = (total[away, part, :] + core_in[away, part, :]).astype(jnp.bfloat16)
            s2_copies[c, h] = send(
                s2_out,
                s2_in,
                s2_sem.at[c, h, 0],
                s2_sem.at[c, h, 1],
                (span, x_mate if h == 0 else y_mate),
            )
            for j in range(2):
                here = 2 * j + my_x if h == 0 else 2 * my_y + j
                kept[j] = total[here, part, :] + core_in[here, part, :]

    def second_axis(c):
        for h in range(2):
            s2_in, kept, s3_out, s3_in = buf[c][7 + h], buf[c][9 + h], buf[c][11 + h], buf[c][13 + h]
            s2_copies[c, h].wait_recv()
            bit = my_y if h == 0 else my_x
            s3_out[...] = kept[1 - bit] + s2_in[1 - bit]
            s3_copies[c, h] = send(
                s3_out,
                s3_in,
                s3_sem.at[c, h, 0],
                s3_sem.at[c, h, 1],
                (span, y_mate if h == 0 else x_mate),
            )

    inner = jnp.logical_and(span >= 1, span <= 2)
    outer = jnp.logical_not(inner)
    near = jnp.where(span < 2, 1 - span, 5 - span)

    def z_copy(c, h, kind):
        z_out, z_one, z_two, z_end = buf[c][15 + h], buf[c][17 + h], buf[c][19 + h], buf[c][21 + h]
        src, dst, other = {
            "in": (z_out, z_one, near),
            "across": (z_out, z_two, 3 - span),
            "back": (z_end, z_end, near),
        }[kind]
        slot_of = {"in": 0, "across": 1, "back": 2}[kind]
        return pltpu.make_async_remote_copy(
            src_ref=src,
            dst_ref=dst,
            send_sem=z_send.at[c, h, slot_of],
            recv_sem=z_recv.at[c, h, slot_of],
            device_id=(other, me),
            device_id_type=MESH,
        )

    def chain_start(c):
        for h in range(2):
            s2_in, kept, s3_in = buf[c][7 + h], buf[c][9 + h], buf[c][13 + h]
            z_out, z_one = buf[c][15 + h], buf[c][17 + h]
            s3_copies[c, h].wait_recv()
            bit = my_y if h == 0 else my_x
            own = kept[bit] + s2_in[bit] + s3_in[...]

            @pl.when(outer)
            def _():
                z_out[...] = own
                z_copy(c, h, "in").start()

            @pl.when(inner)
            def _():
                z_copy(c, h, "in").wait_recv()
                z_out[...] = own + z_one[...]
                z_copy(c, h, "across").start()

    def chain_middle(c):
        for h in range(2):
            z_out, z_two, z_end = buf[c][15 + h], buf[c][19 + h], buf[c][21 + h]

            @pl.when(inner)
            def _():
                z_copy(c, h, "across").wait_recv()
                z_end[...] = z_out[...] + z_two[...]
                z_copy(c, h, "back").start()

    def finish(c):
        lo, hi = chunks[c]
        for h in range(2):
            z_end = buf[c][21 + h]

            @pl.when(outer)
            def _():
                z_copy(c, h, "back").wait_recv()

            part = pl.ds(h * half, half)
            new = adam_update(
                z_end[...], master[part, lo:hi], one[part, lo:hi], two[part, lo:hi]
            )
            out_master[part, lo:hi] = new[0]
            out_first[part, lo:hi] = new[1]
            out_second[part, lo:hi] = new[2]

    form(0)
    first_axis(0)
    second_axis(0)
    chain_start(0)
    form(1)
    first_axis(1)
    chain_middle(0)
    form(2)
    second_axis(1)
    first_axis(2)
    chain_start(1)
    second_axis(2)
    for i in (7, 8, 9):
        loads[i].wait()
    finish(0)
    chain_middle(1)
    chain_start(2)
    finish(1)
    chain_middle(2)
    finish(2)

    for copy in a2a:
        copy.wait_send()
    for c in range(len(chunks)):
        core_copies[c].wait_send()
        for h in range(2):
            s2_copies[c, h].wait_send()
            s3_copies[c, h].wait_send()

            @pl.when(outer)
            def _():
                z_copy(c, h, "in").wait_send()

            @pl.when(inner)
            def _():
                z_copy(c, h, "across").wait_send()
                z_copy(c, h, "back").wait_send()


def kernel_body(
    tokens,
    out_proj,
    phi_mean,
    phi_rotate,
    destinations,
    student_hidden,
    adaptor,
    master,
    moment_one,
    moment_two,
):
    rows = tokens.shape[0]
    slots, width = student_hidden.shape
    features = adaptor.shape[1]
    block = width // SHARDS
    half = block // 2
    chunks = chunks_of(features)
    bf16, f32 = jnp.bfloat16, jnp.float32
    dest = destinations.reshape(1, rows)
    inputs = (
        tokens,
        out_proj,
        phi_mean,
        phi_rotate.T,
        dest,
        student_hidden,
        adaptor.T,
        master,
        moment_one,
        moment_two,
    )
    scratch = [pltpu.VMEM(a.shape, a.dtype) for a in inputs]
    scratch += [
        pltpu.VMEM((slots, width), bf16),
        pltpu.VMEM((width, slots), bf16),
        pltpu.VMEM((slots, features), f32),
    ]
    for lo, hi in chunks:
        wide = hi - lo
        scratch += [pltpu.VMEM((slots, wide), bf16)] * 2
        scratch += [pltpu.VMEM((4, block, wide), bf16)] * 2
        scratch += [pltpu.VMEM((4, block, wide), f32)]
        scratch += [pltpu.VMEM((2, half, wide), bf16)] * 4
        scratch += [pltpu.VMEM((2, half, wide), f32)] * 2
        scratch += [pltpu.VMEM((half, wide), f32)] * 12
    n = len(chunks)
    dma = pltpu.SemaphoreType.DMA
    scratch += [
        dma((len(inputs),)),
        dma((n, SPANS - 1)),
        dma((n, SPANS - 1)),
        dma((n, 2)),
        dma((n, 2, 2)),
        dma((n, 2, 2)),
        dma((n, 2, 3)),
        dma((n, 2, 3)),
    ]
    flops = 2 * (rows * tokens.shape[1] * (tokens.shape[1] + features) + 2 * slots * width * features)
    return pl.pallas_call(
        functools.partial(step_kernel, chunks),
        out_shape=[jax.ShapeDtypeStruct(master.shape, f32)] * 3,
        in_specs=[pl.BlockSpec(memory_space=pl.ANY)] * len(inputs),
        out_specs=[pl.BlockSpec(memory_space=pltpu.VMEM)] * 3,
        scratch_shapes=scratch,
        compiler_params=pltpu.CompilerParams(
            collective_id=0, has_side_effects=True, vmem_limit_bytes=62 * 2**20
        ),
        cost_estimate=pl.CostEstimate(
            flops=flops, bytes_accessed=10 * 2**20, transcendentals=slots * width
        ),
    )(*inputs)


def solution(mesh):
    in_specs = (
        P(("span", "shard"), None),
        P(),
        P(),
        P(),
        P(("span", "shard"), None),
        P(("span", "shard"), None),
        P(),
        P("shard", None),
        P("shard", None),
        P("shard", None),
    )
    out_specs = (P("shard", None), P("shard", None), P("shard", None))
    tuned = mesh.shape["span"] == SPANS and mesh.shape["shard"] == SHARDS
    body = kernel_body if tuned else general_body
    return jax.shard_map(body, mesh=mesh, in_specs=in_specs, out_specs=out_specs, check_vma=False)
```

```python
import functools

import jax
import jax.numpy as jnp
from jax import lax
from jax.experimental import pallas as pl
from jax.experimental.pallas import tpu as pltpu
from jax.sharding import PartitionSpec as P

ADAM_STEP = 1000


beta_first = 0.9
beta_second = 0.999
adam_epsilon = 1e-08
decay_rate = 0.05
learn_rate = 0.001

EMPTY = 2.0**100
EMPTY_TEST = 2.0**90
MESH = pl.DeviceIdType.MESH


def adam_update(gradient, master, moment_one, moment_two):
    first_new = beta_first * moment_one + (1.0 - beta_first) * gradient
    second_new = beta_second * moment_two + (1.0 - beta_second) * gradient * gradient
    bias_first = 1.0 - beta_first**ADAM_STEP
    bias_second = 1.0 - beta_second**ADAM_STEP
    update_dir = (
        first_new / bias_first / (jnp.sqrt(second_new / bias_second) + adam_epsilon)
        + decay_rate * master
    )
    return (master - learn_rate * update_dir, first_new, second_new)


def route_slots(destinations, span_count, capacity):
    target_span = destinations[:, 0]
    span_ids = jnp.arange(span_count, dtype=jnp.int32)
    one_hot = (target_span[:, None] == span_ids[None, :]).astype(jnp.int32)
    before = jnp.cumsum(one_hot, axis=0) - one_hot
    slot_rank = jnp.sum(before * one_hot, axis=1)
    return target_span * capacity + slot_rank


def general_body(
    tokens,
    out_proj,
    phi_mean,
    phi_rotate,
    destinations,
    student_hidden,
    adaptor,
    master,
    moment_one,
    moment_two,
):
    span_count = lax.axis_size("span")
    slots = student_hidden.shape[0]
    capacity = slots // span_count
    features = adaptor.shape[1]
    projected = (jnp.dot(tokens, out_proj, preferred_element_type=jnp.float32) - phi_mean).astype(
        jnp.bfloat16
    )
    target = jnp.dot(projected, phi_rotate, preferred_element_type=jnp.float32).astype(jnp.bfloat16)
    slot_ids = route_slots(destinations, span_count, capacity)
    placed = jnp.full((slots, features), EMPTY, jnp.bfloat16).at[slot_ids].set(target)
    arrived = lax.all_to_all(
        placed.reshape(span_count, capacity, features), "span", split_axis=0, concat_axis=0, tiled=True
    ).reshape(slots, features)
    activated = jax.nn.gelu(student_hidden.astype(jnp.float32), approximate=False).astype(jnp.bfloat16)
    predicted = jnp.dot(activated, adaptor, preferred_element_type=jnp.float32)
    wanted = arrived.astype(jnp.float32)
    scaled_error = jnp.where(wanted > EMPTY_TEST, 0.0, (predicted - wanted) / features).astype(
        jnp.bfloat16
    )
    contract = (((0,), (0,)), ((), ()))
    partial_sum = lax.psum_scatter(
        lax.dot_general(activated, scaled_error, contract, preferred_element_type=jnp.float32),
        "shard",
        scatter_dimension=0,
        tiled=True,
    )
    return adam_update(lax.psum(partial_sum, "span"), master, moment_one, moment_two)


SPANS = 4
SHARDS = 8


def chunks_of(features):
    last = features // 128 * 128
    first = last // 256 * 128
    return ((0, first), (first, last), (last, features))


def dot(a, b):
    return jnp.dot(a, b, preferred_element_type=jnp.float32)


def dot_t(a, b):
    return lax.dot_general(a, b, (((1,), (1,)), ((), ())), preferred_element_type=jnp.float32)


def encode(values, codes, scale):
    top = jnp.max(jnp.max(jnp.abs(values), axis=0, keepdims=True), axis=1, keepdims=True)
    top = jnp.maximum(top, 1e-30)
    codes[...] = jnp.round(values * (32000.0 / top)).astype(jnp.int32).astype(jnp.int16)
    scale[...] = jnp.broadcast_to(top * (1.0 / 32000.0), scale.shape)


def decode(codes, scale):
    return codes[...].astype(jnp.int32).astype(jnp.float32) * scale[0:1, 0:1]


def step_kernel(
    chunks,
    tokens_hbm,
    proj_hbm,
    mean_hbm,
    rotate_hbm,
    dest_hbm,
    hidden_hbm,
    adaptor_hbm,
    out,
    tokens,
    proj,
    mean,
    rotate,
    dest,
    hidden,
    adaptor,
    act,
    act_t,
    pred,
    *rest,
):
    per_chunk, (load_sem, a2a_send, a2a_recv, core_sem, s2_sem, s3_sem, z_send, z_recv) = (
        rest[:-8],
        rest[-8:],
    )
    count = len(per_chunk) // len(chunks)
    buf = [per_chunk[c * count : (c + 1) * count] for c in range(len(chunks))]

    span = lax.axis_index("span")
    me = lax.axis_index("shard")
    core = lax.rem(me, 2)
    my_x = lax.rem(me // 2, 2)
    my_y = me // 4
    core_mate = me + 1 - 2 * core
    x_mate = me + 2 - 4 * my_x
    y_mate = me + 4 - 8 * my_y

    slots, width = hidden.shape
    rows = tokens.shape[0]
    features = adaptor.shape[0]
    cap = slots // SPANS
    block = width // SHARDS
    half = block // 2

    pairs = (
        (tokens_hbm, tokens),
        (proj_hbm, proj),
        (mean_hbm, mean),
        (dest_hbm, dest),
        (rotate_hbm, rotate),
        (hidden_hbm, hidden),
        (adaptor_hbm, adaptor),
    )
    loads = [pltpu.make_async_copy(s, d, load_sem.at[i]) for i, (s, d) in enumerate(pairs)]
    for i in (0, 1, 2, 3, 4):
        loads[i].start()

    barrier = pltpu.get_barrier_semaphore()
    for step in range(1, SPANS):
        pl.semaphore_signal(
            barrier, inc=1, device_id=(lax.rem(span + step, SPANS), me), device_id_type=MESH
        )
    for mate in (core_mate, x_mate, y_mate):
        pl.semaphore_signal(barrier, inc=1, device_id=(span, mate), device_id_type=MESH)

    loads[3].wait()
    wanted = dest[...]
    span_ids = lax.broadcasted_iota(jnp.int32, (16, rows), 0)
    one_hot = jnp.where(span_ids == wanted, 1.0, 0.0)
    earlier = jnp.where(
        lax.broadcasted_iota(jnp.int32, (rows, rows), 0)
        < lax.broadcasted_iota(jnp.int32, (rows, rows), 1),
        1.0,
        0.0,
    ).astype(jnp.bfloat16)
    before = dot(one_hot.astype(jnp.bfloat16), earlier)
    rank = jnp.sum(before * one_hot, axis=0, keepdims=True).astype(jnp.int32)
    slot = wanted * cap + rank
    place = jnp.where(lax.broadcasted_iota(jnp.int32, (slots, rows), 0) == slot, 1.0, 0.0)
    empty = (1.0 - jnp.sum(place, axis=1, keepdims=True)) * EMPTY
    place = place.astype(jnp.bfloat16)

    for i in (0, 1, 2):
        loads[i].wait()
    projected = (dot(tokens[...], proj[...]) - mean[...].reshape(1, -1)).astype(jnp.bfloat16)
    for i in (5, 6):
        loads[i].start()
    loads[4].wait()
    pl.semaphore_wait(barrier, SPANS - 1 + 3)

    a2a = []
    for c, (lo, hi) in enumerate(chunks):
        t_send, t_recv = buf[c][0], buf[c][1]
        target = dot_t(projected, rotate[lo:hi, :]).astype(jnp.bfloat16)
        t_send[...] = (dot(place, target) + empty).astype(jnp.bfloat16)
        for step in (2, 3, 1):
            other = lax.rem(span + step, SPANS)
            copy = pltpu.make_async_remote_copy(
                src_ref=t_send.at[pl.ds(pl.multiple_of(other * cap, 16), cap)],
                dst_ref=t_recv.at[pl.ds(pl.multiple_of(span * cap, 16), cap)],
                send_sem=a2a_send.at[c, step - 1],
                recv_sem=a2a_recv.at[c, step - 1],
                device_id=(other, me),
                device_id_type=MESH,
            )
            copy.start()
            a2a.append(copy)
        mine = pl.ds(pl.multiple_of(span * cap, 16), cap)
        t_recv[mine, :] = t_send[mine, :]

    loads[5].wait()
    for j in range(0, width, 128):
        x = hidden[:, j : j + 128].astype(jnp.float32)
        a = (0.5 * x * (1.0 + lax.erf(x * (0.5**0.5)))).astype(jnp.bfloat16)
        act[:, j : j + 128] = a
        act_t[j : j + 128, :] = a.T
    loads[6].wait()
    pred[...] = dot_t(act[...], adaptor[...])

    sends = []

    def send(src, dst, send_sem, recv_sem, device):
        copy = pltpu.make_async_remote_copy(
            src_ref=src,
            dst_ref=dst,
            send_sem=send_sem,
            recv_sem=recv_sem,
            device_id=device,
            device_id_type=MESH,
        )
        copy.start()
        return copy

    class Pair:
        def __init__(self, c, src, dst, sems, device):
            self.copies = [
                pltpu.make_async_remote_copy(
                    src_ref=buf[c][src + 12 * i],
                    dst_ref=buf[c][dst + 12 * i],
                    send_sem=sems[i],
                    recv_sem=sems[2 + i],
                    device_id=device,
                    device_id_type=MESH,
                )
                for i in range(2)
            ]

        def start(self):
            for copy in self.copies:
                copy.start()

        def wait_recv(self):
            for copy in self.copies:
                copy.wait_recv()

        def wait_send(self):
            for copy in self.copies:
                copy.wait_send()

    def put(values, c, at):
        encode(values, buf[c][at], buf[c][at + 12])

    def get(c, at):
        return decode(buf[c][at], buf[c][at + 12])

    core_copies = {}
    s2_copies = {}
    s3_copies = {}

    def gradient_block(index, error):
        start = pl.multiple_of(index * block, 16)
        return dot(act_t[pl.ds(start, block), :], error)

    def form(c):
        lo, hi = chunks[c]
        t_recv, core_out, core_in, total = buf[c][1], buf[c][2], buf[c][3], buf[c][4]
        for copy in a2a[3 * c : 3 * c + 3]:
            copy.wait_recv()
        t = t_recv[...].astype(jnp.float32)
        error = jnp.where(t > EMPTY_TEST, 0.0, (pred[:, lo:hi] - t) * (1.0 / features)).astype(
            jnp.bfloat16
        )
        for j in range(4):
            core_out[j] = gradient_block(2 * j + 1 - core, error).astype(jnp.bfloat16)
        core_copies[c] = send(
            core_out, core_in, core_sem.at[c, 0], core_sem.at[c, 1], (span, core_mate)
        )
        for j in range(4):
            total[j] = gradient_block(2 * j + core, error)

    def first_axis(c):
        core_in, total = buf[c][3], buf[c][4]
        core_copies[c].wait_recv()
        for h in range(2):
            s2_out, s2_in, kept = buf[c][5 + h], buf[c][7 + h], buf[c][9 + h]
            part = pl.ds(h * half, half)
            for j in range(2):
                away = 2 * j + 1 - my_x if h == 0 else 2 * (1 - my_y) + j
                s2_out[j] = (total[away, part, :] + core_in[away, part, :]).astype(jnp.bfloat16)
            s2_copies[c, h] = send(
                s2_out,
                s2_in,
                s2_sem.at[c, h, 0],
                s2_sem.at[c, h, 1],
                (span, x_mate if h == 0 else y_mate),
            )
            for j in range(2):
                here = 2 * j + my_x if h == 0 else 2 * my_y + j
                kept[j] = total[here, part, :] + core_in[here, part, :]

    def second_axis(c):
        for h in range(2):
            s2_in, kept = buf[c][7 + h], buf[c][9 + h]
            s2_copies[c, h].wait_recv()
            bit = my_y if h == 0 else my_x
            put(kept[1 - bit] + s2_in[1 - bit], c, 11 + h)
            s3_copies[c, h] = Pair(
                c,
                11 + h,
                13 + h,
                [s3_sem.at[c, h, i] for i in range(4)],
                (span, y_mate if h == 0 else x_mate),
            )
            s3_copies[c, h].start()

    inner = jnp.logical_and(span >= 1, span <= 2)
    outer = jnp.logical_not(inner)
    near = jnp.where(span < 2, 1 - span, 5 - span)

    def z_copy(c, h, kind):
        src, dst, other, at = {
            "in": (15, 17, near, 0),
            "across": (15, 19, 3 - span, 2),
            "back": (21, 21, near, 4),
        }[kind]
        sems = [z_send.at[c, h, at + i] for i in range(2)] + [z_recv.at[c, h, at + i] for i in range(2)]
        return Pair(c, src + h, dst + h, sems, (other, me))

    def chain_start(c):
        for h in range(2):
            s2_in, kept = buf[c][7 + h], buf[c][9 + h]
            s3_copies[c, h].wait_recv()
            bit = my_y if h == 0 else my_x
            own = kept[bit] + s2_in[bit] + get(c, 13 + h)

            @pl.when(outer)
            def _():
                put(own, c, 15 + h)
                z_copy(c, h, "in").start()

            @pl.when(inner)
            def _():
                z_copy(c, h, "in").wait_recv()
                put(own + get(c, 17 + h), c, 15 + h)
                z_copy(c, h, "across").start()

    def chain_middle(c):
        for h in range(2):

            @pl.when(inner)
            def _():
                z_copy(c, h, "across").wait_recv()
                mine, other = get(c, 15 + h), get(c, 19 + h)
                low = jnp.where(span < 2, mine, other)
                high = jnp.where(span < 2, other, mine)
                put(low + high, c, 21 + h)
                z_copy(c, h, "back").start()

    def finish(c):
        lo, hi = chunks[c]
        for h in range(2):

            @pl.when(outer)
            def _():
                z_copy(c, h, "back").wait_recv()

            out[h * half : (h + 1) * half, lo:hi] = get(c, 21 + h)

    form(0)
    first_axis(0)
    second_axis(0)
    chain_start(0)
    form(1)
    first_axis(1)
    chain_middle(0)
    form(2)
    second_axis(1)
    first_axis(2)
    chain_start(1)
    second_axis(2)
    finish(0)
    chain_middle(1)
    chain_start(2)
    finish(1)
    chain_middle(2)
    finish(2)

    for copy in a2a:
        copy.wait_send()
    for c in range(len(chunks)):
        core_copies[c].wait_send()
        for h in range(2):
            s2_copies[c, h].wait_send()
            s3_copies[c, h].wait_send()

            @pl.when(outer)
            def _():
                z_copy(c, h, "in").wait_send()

            @pl.when(inner)
            def _():
                z_copy(c, h, "across").wait_send()
                z_copy(c, h, "back").wait_send()


def kernel_body(
    tokens,
    out_proj,
    phi_mean,
    phi_rotate,
    destinations,
    student_hidden,
    adaptor,
    master,
    moment_one,
    moment_two,
):
    rows = tokens.shape[0]
    slots, width = student_hidden.shape
    features = adaptor.shape[1]
    block = width // SHARDS
    half = block // 2
    chunks = chunks_of(features)
    bf16, f32 = jnp.bfloat16, jnp.float32
    dest = destinations.reshape(1, rows)
    inputs = (
        tokens,
        out_proj,
        phi_mean,
        phi_rotate.T,
        dest,
        student_hidden,
        adaptor.T,
    )
    scratch = [pltpu.VMEM(a.shape, a.dtype) for a in inputs]
    scratch += [
        pltpu.VMEM((slots, width), bf16),
        pltpu.VMEM((width, slots), bf16),
        pltpu.VMEM((slots, features), f32),
    ]
    for lo, hi in chunks:
        wide = hi - lo
        scratch += [pltpu.VMEM((slots, wide), bf16)] * 2
        scratch += [pltpu.VMEM((4, block, wide), bf16)] * 2
        scratch += [pltpu.VMEM((4, block, wide), f32)]
        scratch += [pltpu.VMEM((2, half, wide), bf16)] * 4
        scratch += [pltpu.VMEM((2, half, wide), f32)] * 2
        scratch += [pltpu.VMEM((half, wide), jnp.int16)] * 12
        scratch += [pltpu.VMEM((8, 128), f32)] * 12
    n = len(chunks)
    dma = pltpu.SemaphoreType.DMA
    scratch += [
        dma((len(inputs),)),
        dma((n, SPANS - 1)),
        dma((n, SPANS - 1)),
        dma((n, 2)),
        dma((n, 2, 2)),
        dma((n, 2, 4)),
        dma((n, 2, 6)),
        dma((n, 2, 6)),
    ]
    flops = 2 * (rows * tokens.shape[1] * (tokens.shape[1] + features) + 2 * slots * width * features)
    gradient = pl.pallas_call(
        functools.partial(step_kernel, chunks),
        out_shape=jax.ShapeDtypeStruct(master.shape, f32),
        in_specs=[pl.BlockSpec(memory_space=pl.ANY)] * len(inputs),
        out_specs=pl.BlockSpec(memory_space=pltpu.VMEM),
        scratch_shapes=scratch,
        compiler_params=pltpu.CompilerParams(
            collective_id=0, has_side_effects=True, vmem_limit_bytes=62 * 2**20
        ),
        cost_estimate=pl.CostEstimate(
            flops=flops, bytes_accessed=10 * 2**20, transcendentals=slots * width
        ),
    )(*inputs)
    return adam_update(gradient, master, moment_one, moment_two)


def solution(mesh):
    in_specs = (
        P(("span", "shard"), None),
        P(),
        P(),
        P(),
        P(("span", "shard"), None),
        P(("span", "shard"), None),
        P(),
        P("shard", None),
        P("shard", None),
        P("shard", None),
    )
    out_specs = (P("shard", None), P("shard", None), P("shard", None))
    tuned = mesh.shape["span"] == SPANS and mesh.shape["shard"] == SHARDS
    body = kernel_body if tuned else general_body
    return jax.shard_map(body, mesh=mesh, in_specs=in_specs, out_specs=out_specs, check_vma=False)
```

```python
import functools

import jax
import jax.numpy as jnp
from jax import lax
from jax.experimental import pallas as pl
from jax.experimental.pallas import tpu as pltpu
from jax.sharding import PartitionSpec as P

ADAM_STEP = 1000


beta_first = 0.9
beta_second = 0.999
adam_epsilon = 1e-08
decay_rate = 0.05
learn_rate = 0.001

EMPTY = 2.0**100
EMPTY_TEST = 2.0**90
MESH = pl.DeviceIdType.MESH


def adam_update(gradient, master, moment_one, moment_two):
    first_new = beta_first * moment_one + (1.0 - beta_first) * gradient
    second_new = beta_second * moment_two + (1.0 - beta_second) * gradient * gradient
    bias_first = 1.0 - beta_first**ADAM_STEP
    bias_second = 1.0 - beta_second**ADAM_STEP
    update_dir = (
        first_new / bias_first / (jnp.sqrt(second_new / bias_second) + adam_epsilon)
        + decay_rate * master
    )
    return (master - learn_rate * update_dir, first_new, second_new)


def route_slots(destinations, span_count, capacity):
    target_span = destinations[:, 0]
    span_ids = jnp.arange(span_count, dtype=jnp.int32)
    one_hot = (target_span[:, None] == span_ids[None, :]).astype(jnp.int32)
    before = jnp.cumsum(one_hot, axis=0) - one_hot
    slot_rank = jnp.sum(before * one_hot, axis=1)
    return target_span * capacity + slot_rank


def general_body(
    tokens,
    out_proj,
    phi_mean,
    phi_rotate,
    destinations,
    student_hidden,
    adaptor,
    master,
    moment_one,
    moment_two,
):
    span_count = lax.axis_size("span")
    slots = student_hidden.shape[0]
    capacity = slots // span_count
    features = adaptor.shape[1]
    projected = (jnp.dot(tokens, out_proj, preferred_element_type=jnp.float32) - phi_mean).astype(
        jnp.bfloat16
    )
    target = jnp.dot(projected, phi_rotate, preferred_element_type=jnp.float32).astype(jnp.bfloat16)
    slot_ids = route_slots(destinations, span_count, capacity)
    placed = jnp.full((slots, features), EMPTY, jnp.bfloat16).at[slot_ids].set(target)
    arrived = lax.all_to_all(
        placed.reshape(span_count, capacity, features), "span", split_axis=0, concat_axis=0, tiled=True
    ).reshape(slots, features)
    activated = jax.nn.gelu(student_hidden.astype(jnp.float32), approximate=False).astype(jnp.bfloat16)
    predicted = jnp.dot(activated, adaptor, preferred_element_type=jnp.float32)
    wanted = arrived.astype(jnp.float32)
    scaled_error = jnp.where(wanted > EMPTY_TEST, 0.0, (predicted - wanted) / features).astype(
        jnp.bfloat16
    )
    contract = (((0,), (0,)), ((), ()))
    partial_sum = lax.psum_scatter(
        lax.dot_general(activated, scaled_error, contract, preferred_element_type=jnp.float32),
        "shard",
        scatter_dimension=0,
        tiled=True,
    )
    return adam_update(lax.psum(partial_sum, "span"), master, moment_one, moment_two)


SPANS = 4
SHARDS = 8


def chunks_of(features):
    return tuple((lo, min(lo + 128, features)) for lo in range(0, features, 128))


def dot(a, b):
    return jnp.dot(a, b, preferred_element_type=jnp.float32)


def dot_t(a, b):
    return lax.dot_general(a, b, (((1,), (1,)), ((), ())), preferred_element_type=jnp.float32)


def encode(values, codes, scale):
    top = jnp.max(jnp.max(jnp.abs(values), axis=0, keepdims=True), axis=1, keepdims=True)
    top = jnp.maximum(top, 1e-30)
    codes[...] = jnp.round(values * (32000.0 / top)).astype(jnp.int32).astype(jnp.int16)
    scale[...] = jnp.broadcast_to(top * (1.0 / 32000.0), scale.shape)


def decode(codes, scale):
    return codes[...].astype(jnp.int32).astype(jnp.float32) * scale[0:1, 0:1]


def step_kernel(
    chunks,
    tokens_hbm,
    proj_hbm,
    mean_hbm,
    rotate_hbm,
    dest_hbm,
    hidden_hbm,
    adaptor_hbm,
    out,
    tokens,
    proj,
    mean,
    rotate,
    dest,
    hidden,
    adaptor,
    act,
    act_t,
    pred,
    *rest,
):
    per_chunk, (load_sem, a2a_send, a2a_recv, core_sem, plane_send, plane_recv, z_sem) = (
        rest[:-7],
        rest[-7:],
    )
    count = len(per_chunk) // len(chunks)
    buf = [per_chunk[c * count : (c + 1) * count] for c in range(len(chunks))]

    span = lax.axis_index("span")
    me = lax.axis_index("shard")
    core = lax.rem(me, 2)
    my_x = lax.rem(me // 2, 2)
    my_y = me // 4
    core_mate = me + 1 - 2 * core
    x_mate = me + 2 - 4 * my_x
    y_mate = me + 4 - 8 * my_y
    cross_mate = y_mate + 2 - 4 * my_x
    plane_mates = (x_mate, y_mate, cross_mate)
    z_mates = (span + 1 - 2 * lax.rem(span, 2), span + 2 - 4 * (span // 2))
    z_low = (lax.rem(span, 2) == 0, span < 2)

    slots, width = hidden.shape
    rows = tokens.shape[0]
    features = adaptor.shape[0]
    cap = slots // SPANS
    block = width // SHARDS

    pairs = (
        (tokens_hbm, tokens),
        (proj_hbm, proj),
        (mean_hbm, mean),
        (dest_hbm, dest),
        (rotate_hbm, rotate),
        (hidden_hbm, hidden),
        (adaptor_hbm, adaptor),
    )
    loads = [pltpu.make_async_copy(s, d, load_sem.at[i]) for i, (s, d) in enumerate(pairs)]
    for i in (0, 1, 2, 3, 4):
        loads[i].start()

    barrier = pltpu.get_barrier_semaphore()
    for step in range(1, SPANS):
        pl.semaphore_signal(
            barrier, inc=1, device_id=(lax.rem(span + step, SPANS), me), device_id_type=MESH
        )
    for mate in (core_mate, *plane_mates):
        pl.semaphore_signal(barrier, inc=1, device_id=(span, mate), device_id_type=MESH)

    loads[3].wait()
    wanted = dest[...]
    span_ids = lax.broadcasted_iota(jnp.int32, (16, rows), 0)
    one_hot = jnp.where(span_ids == wanted, 1.0, 0.0)
    earlier = jnp.where(
        lax.broadcasted_iota(jnp.int32, (rows, rows), 0)
        < lax.broadcasted_iota(jnp.int32, (rows, rows), 1),
        1.0,
        0.0,
    ).astype(jnp.bfloat16)
    before = dot(one_hot.astype(jnp.bfloat16), earlier)
    rank = jnp.sum(before * one_hot, axis=0, keepdims=True).astype(jnp.int32)
    slot = wanted * cap + rank
    place = jnp.where(lax.broadcasted_iota(jnp.int32, (slots, rows), 0) == slot, 1.0, 0.0)
    empty = (1.0 - jnp.sum(place, axis=1, keepdims=True)) * EMPTY
    place = place.astype(jnp.bfloat16)

    for i in (0, 1, 2):
        loads[i].wait()
    projected = (dot(tokens[...], proj[...]) - mean[...].reshape(1, -1)).astype(jnp.bfloat16)
    for i in (5, 6):
        loads[i].start()
    loads[4].wait()
    pl.semaphore_wait(barrier, SPANS - 1 + 4)

    a2a = []
    for c, (lo, hi) in enumerate(chunks):
        t_send, t_recv = buf[c][0], buf[c][1]
        target = dot_t(projected, rotate[lo:hi, :]).astype(jnp.bfloat16)
        t_send[...] = (dot(place, target) + empty).astype(jnp.bfloat16)
        for step in (2, 3, 1):
            other = lax.rem(span + step, SPANS)
            copy = pltpu.make_async_remote_copy(
                src_ref=t_send.at[pl.ds(pl.multiple_of(other * cap, 16), cap)],
                dst_ref=t_recv.at[pl.ds(pl.multiple_of(span * cap, 16), cap)],
                send_sem=a2a_send.at[c, step - 1],
                recv_sem=a2a_recv.at[c, step - 1],
                device_id=(other, me),
                device_id_type=MESH,
            )
            copy.start()
            a2a.append(copy)
        mine = pl.ds(pl.multiple_of(span * cap, 16), cap)
        t_recv[mine, :] = t_send[mine, :]

    loads[5].wait()
    for j in range(0, width, 128):
        x = hidden[:, j : j + 128].astype(jnp.float32)
        a = (0.5 * x * (1.0 + lax.erf(x * (0.5**0.5)))).astype(jnp.bfloat16)
        act[:, j : j + 128] = a
        act_t[j : j + 128, :] = a.T
    loads[6].wait()
    pred[...] = dot_t(act[...], adaptor[...])

    sends = []

    def send(src, dst, send_sem, recv_sem, device):
        copy = pltpu.make_async_remote_copy(
            src_ref=src,
            dst_ref=dst,
            send_sem=send_sem,
            recv_sem=recv_sem,
            device_id=device,
            device_id_type=MESH,
        )
        copy.start()
        return copy

    class Pair:
        def __init__(self, c, src, dst, sems, device):
            self.copies = [
                pltpu.make_async_remote_copy(
                    src_ref=buf[c][src + 4 * i],
                    dst_ref=buf[c][dst + 4 * i],
                    send_sem=sems[i],
                    recv_sem=sems[2 + i],
                    device_id=device,
                    device_id_type=MESH,
                )
                for i in range(2)
            ]

        def start(self):
            for copy in self.copies:
                copy.start()

        def wait_recv(self):
            for copy in self.copies:
                copy.wait_recv()

        def wait_send(self):
            for copy in self.copies:
                copy.wait_send()

    def put(values, c, at):
        encode(values, buf[c][at], buf[c][at + 4])

    def get(c, at):
        return decode(buf[c][at], buf[c][at + 4])

    core_copies = {}
    plane_copies = {}
    z_copies = {}

    def gradient_block(index, error):
        start = pl.multiple_of(index * block, 16)
        return dot(act_t[pl.ds(start, block), :], error)

    def form(c):
        lo, hi = chunks[c]
        t_recv, core_out, core_in, total = buf[c][1], buf[c][2], buf[c][3], buf[c][4]
        for copy in a2a[3 * c : 3 * c + 3]:
            copy.wait_recv()
        t = t_recv[...].astype(jnp.float32)
        error = jnp.where(t > EMPTY_TEST, 0.0, (pred[:, lo:hi] - t) * (1.0 / features)).astype(
            jnp.bfloat16
        )
        for j in range(4):
            core_out[j] = gradient_block(2 * j + 1 - core, error).astype(jnp.bfloat16)
        core_copies[c] = send(
            core_out, core_in, core_sem.at[c, 0], core_sem.at[c, 1], (span, core_mate)
        )
        for j in range(4):
            total[j] = gradient_block(2 * j + core, error)

    def plane(c):
        core_in, total, plane_out, plane_in = buf[c][3], buf[c][4], buf[c][5], buf[c][6]
        core_copies[c].wait_recv()
        for j, mate in enumerate(plane_mates):
            away = mate // 2
            plane_out[j] = (total[away] + core_in[away]).astype(jnp.bfloat16)
            plane_copies[c, j] = send(
                plane_out.at[j],
                plane_in.at[j],
                plane_send.at[c, j],
                plane_recv.at[c, j],
                (span, mate),
            )

    def z_send(c, stage):
        at = 7 + 2 * stage
        z_copies[c, stage] = Pair(
            c, at, at + 1, [z_sem.at[c, stage, i] for i in range(4)], (z_mates[stage], me)
        )
        z_copies[c, stage].start()

    def z_sum(c, stage):
        at = 7 + 2 * stage
        z_copies[c, stage].wait_recv()
        mine, other = get(c, at), get(c, at + 1)
        low = jnp.where(z_low[stage], mine, other)
        high = jnp.where(z_low[stage], other, mine)
        return low + high

    def first_z(c):
        core_in, total, plane_in = buf[c][3], buf[c][4], buf[c][6]
        here = me // 2
        own = total[here] + core_in[here]
        for j in range(3):
            plane_copies[c, j].wait_recv()
            own = own + plane_in[j]
        put(own, c, 7)
        z_send(c, 0)

    def second_z(c):
        put(z_sum(c, 0), c, 9)
        z_send(c, 1)

    def finish(c):
        lo, hi = chunks[c]
        out[:, lo:hi] = z_sum(c, 1)

    n = len(chunks)
    for c in range(n):
        form(c)
        if c >= 1:
            first_z(c - 1)
        if c >= 2:
            second_z(c - 2)
        plane(c)
        if c >= 3:
            finish(c - 3)
    second_z(n - 2)
    first_z(n - 1)
    finish(n - 3)
    finish(n - 2)
    second_z(n - 1)
    finish(n - 1)

    for copy in a2a:
        copy.wait_send()
    for group in (core_copies, plane_copies, z_copies):
        for copy in group.values():
            copy.wait_send()


def kernel_body(
    tokens,
    out_proj,
    phi_mean,
    phi_rotate,
    destinations,
    student_hidden,
    adaptor,
    master,
    moment_one,
    moment_two,
):
    rows = tokens.shape[0]
    slots, width = student_hidden.shape
    features = adaptor.shape[1]
    block = width // SHARDS
    chunks = chunks_of(features)
    bf16, f32 = jnp.bfloat16, jnp.float32
    dest = destinations.reshape(1, rows)
    inputs = (
        tokens,
        out_proj,
        phi_mean,
        phi_rotate.T,
        dest,
        student_hidden,
        adaptor.T,
    )
    scratch = [pltpu.VMEM(a.shape, a.dtype) for a in inputs]
    scratch += [
        pltpu.VMEM((slots, width), bf16),
        pltpu.VMEM((width, slots), bf16),
        pltpu.VMEM((slots, features), f32),
    ]
    for lo, hi in chunks:
        wide = hi - lo
        scratch += [pltpu.VMEM((slots, wide), bf16)] * 2
        scratch += [pltpu.VMEM((4, block, wide), bf16)] * 2
        scratch += [pltpu.VMEM((4, block, wide), f32)]
        scratch += [pltpu.VMEM((3, block, wide), bf16)] * 2
        scratch += [pltpu.VMEM((block, wide), jnp.int16)] * 4
        scratch += [pltpu.VMEM((8, 128), f32)] * 4
    n = len(chunks)
    dma = pltpu.SemaphoreType.DMA
    scratch += [
        dma((len(inputs),)),
        dma((n, SPANS - 1)),
        dma((n, SPANS - 1)),
        dma((n, 2)),
        dma((n, 3)),
        dma((n, 3)),
        dma((n, 2, 4)),
    ]
    flops = 2 * (rows * tokens.shape[1] * (tokens.shape[1] + features) + 2 * slots * width * features)
    gradient = pl.pallas_call(
        functools.partial(step_kernel, chunks),
        out_shape=jax.ShapeDtypeStruct(master.shape, f32),
        in_specs=[pl.BlockSpec(memory_space=pl.ANY)] * len(inputs),
        out_specs=pl.BlockSpec(memory_space=pltpu.VMEM),
        scratch_shapes=scratch,
        compiler_params=pltpu.CompilerParams(
            collective_id=0, has_side_effects=True, vmem_limit_bytes=62 * 2**20
        ),
        cost_estimate=pl.CostEstimate(
            flops=flops, bytes_accessed=10 * 2**20, transcendentals=slots * width
        ),
    )(*inputs)
    return adam_update(gradient, master, moment_one, moment_two)


def solution(mesh):
    in_specs = (
        P(("span", "shard"), None),
        P(),
        P(),
        P(),
        P(("span", "shard"), None),
        P(("span", "shard"), None),
        P(),
        P("shard", None),
        P("shard", None),
        P("shard", None),
    )
    out_specs = (P("shard", None), P("shard", None), P("shard", None))
    tuned = mesh.shape["span"] == SPANS and mesh.shape["shard"] == SHARDS
    body = kernel_body if tuned else general_body
    return jax.shard_map(body, mesh=mesh, in_specs=in_specs, out_specs=out_specs, check_vma=False)
```

```python
import functools

import jax
import jax.numpy as jnp
from jax import lax
from jax.experimental import pallas as pl
from jax.experimental.pallas import tpu as pltpu
from jax.sharding import PartitionSpec as P

ADAM_STEP = 1000


beta_first = 0.9
beta_second = 0.999
adam_epsilon = 1e-08
decay_rate = 0.05
learn_rate = 0.001

EMPTY = 2.0**100
EMPTY_TEST = 2.0**90
MESH = pl.DeviceIdType.MESH


def adam_update(gradient, master, moment_one, moment_two):
    first_new = beta_first * moment_one + (1.0 - beta_first) * gradient
    second_new = beta_second * moment_two + (1.0 - beta_second) * gradient * gradient
    bias_first = 1.0 - beta_first**ADAM_STEP
    bias_second = 1.0 - beta_second**ADAM_STEP
    update_dir = (
        first_new / bias_first / (jnp.sqrt(second_new / bias_second) + adam_epsilon)
        + decay_rate * master
    )
    return (master - learn_rate * update_dir, first_new, second_new)


def route_slots(destinations, span_count, capacity):
    target_span = destinations[:, 0]
    span_ids = jnp.arange(span_count, dtype=jnp.int32)
    one_hot = (target_span[:, None] == span_ids[None, :]).astype(jnp.int32)
    before = jnp.cumsum(one_hot, axis=0) - one_hot
    slot_rank = jnp.sum(before * one_hot, axis=1)
    return target_span * capacity + slot_rank


def general_body(
    tokens,
    out_proj,
    phi_mean,
    phi_rotate,
    destinations,
    student_hidden,
    adaptor,
    master,
    moment_one,
    moment_two,
):
    span_count = lax.axis_size("span")
    slots = student_hidden.shape[0]
    capacity = slots // span_count
    features = adaptor.shape[1]
    projected = (jnp.dot(tokens, out_proj, preferred_element_type=jnp.float32) - phi_mean).astype(
        jnp.bfloat16
    )
    target = jnp.dot(projected, phi_rotate, preferred_element_type=jnp.float32).astype(jnp.bfloat16)
    slot_ids = route_slots(destinations, span_count, capacity)
    placed = jnp.full((slots, features), EMPTY, jnp.bfloat16).at[slot_ids].set(target)
    arrived = lax.all_to_all(
        placed.reshape(span_count, capacity, features), "span", split_axis=0, concat_axis=0, tiled=True
    ).reshape(slots, features)
    activated = jax.nn.gelu(student_hidden.astype(jnp.float32), approximate=False).astype(jnp.bfloat16)
    predicted = jnp.dot(activated, adaptor, preferred_element_type=jnp.float32)
    wanted = arrived.astype(jnp.float32)
    scaled_error = jnp.where(wanted > EMPTY_TEST, 0.0, (predicted - wanted) / features).astype(
        jnp.bfloat16
    )
    contract = (((0,), (0,)), ((), ()))
    partial_sum = lax.psum_scatter(
        lax.dot_general(activated, scaled_error, contract, preferred_element_type=jnp.float32),
        "shard",
        scatter_dimension=0,
        tiled=True,
    )
    return adam_update(lax.psum(partial_sum, "span"), master, moment_one, moment_two)


SPANS = 4
SHARDS = 8


def chunks_of(features):
    return tuple((lo, min(lo + 128, features)) for lo in range(0, features, 128))


def dot(a, b):
    return jnp.dot(a, b, preferred_element_type=jnp.float32)


def dot_t(a, b):
    return lax.dot_general(a, b, (((1,), (1,)), ((), ())), preferred_element_type=jnp.float32)


def encode(values, codes, scale):
    top = jnp.max(jnp.max(jnp.abs(values), axis=0, keepdims=True), axis=1, keepdims=True)
    top = jnp.maximum(top, 1e-30)
    codes[...] = jnp.round(values * (32000.0 / top)).astype(jnp.int32).astype(jnp.int16)
    scale[...] = jnp.broadcast_to(top * (1.0 / 32000.0), scale.shape)


def decode(codes, scale):
    return codes[...].astype(jnp.int32).astype(jnp.float32) * scale[0:1, 0:1]


def step_kernel(
    chunks,
    tokens_hbm,
    proj_hbm,
    mean_hbm,
    rotate_hbm,
    dest_hbm,
    hidden_hbm,
    adaptor_hbm,
    out,
    tokens,
    proj,
    mean,
    rotate,
    dest,
    hidden,
    adaptor,
    act,
    act_t,
    pred,
    *rest,
):
    per_chunk, (load_sem, a2a_send, a2a_recv, core_sem, plane_send, plane_recv, z_sem) = (
        rest[:-7],
        rest[-7:],
    )
    count = len(per_chunk) // len(chunks)
    buf = [per_chunk[c * count : (c + 1) * count] for c in range(len(chunks))]

    span = lax.axis_index("span")
    me = lax.axis_index("shard")
    core = lax.rem(me, 2)
    my_x = lax.rem(me // 2, 2)
    my_y = me // 4
    core_mate = me + 1 - 2 * core
    x_mate = me + 2 - 4 * my_x
    y_mate = me + 4 - 8 * my_y
    cross_mate = y_mate + 2 - 4 * my_x
    plane_mates = (x_mate, y_mate, cross_mate)
    z_mates = (span + 1 - 2 * lax.rem(span, 2), span + 2 - 4 * (span // 2))

    slots, width = hidden.shape
    rows = tokens.shape[0]
    features = adaptor.shape[0]
    cap = slots // SPANS
    block = width // SHARDS
    group = width // 2
    half = block // 2

    pairs = (
        (tokens_hbm, tokens),
        (proj_hbm, proj),
        (mean_hbm, mean),
        (dest_hbm, dest),
        (rotate_hbm, rotate),
        (hidden_hbm, hidden),
        (adaptor_hbm, adaptor),
    )
    loads = [pltpu.make_async_copy(s, d, load_sem.at[i]) for i, (s, d) in enumerate(pairs)]
    for i in (0, 1, 2, 3, 4):
        loads[i].start()

    barrier = pltpu.get_barrier_semaphore()
    for step in range(1, SPANS):
        pl.semaphore_signal(
            barrier, inc=1, device_id=(lax.rem(span + step, SPANS), me), device_id_type=MESH
        )
    for mate in (core_mate, *plane_mates):
        pl.semaphore_signal(barrier, inc=1, device_id=(span, mate), device_id_type=MESH)

    loads[3].wait()
    wanted = dest[...]
    span_ids = lax.broadcasted_iota(jnp.int32, (16, rows), 0)
    one_hot = jnp.where(span_ids == wanted, 1.0, 0.0)
    earlier = jnp.where(
        lax.broadcasted_iota(jnp.int32, (rows, rows), 0)
        < lax.broadcasted_iota(jnp.int32, (rows, rows), 1),
        1.0,
        0.0,
    ).astype(jnp.bfloat16)
    before = dot(one_hot.astype(jnp.bfloat16), earlier)
    rank = jnp.sum(before * one_hot, axis=0, keepdims=True).astype(jnp.int32)
    slot = wanted * cap + rank
    place = jnp.where(lax.broadcasted_iota(jnp.int32, (slots, rows), 0) == slot, 1.0, 0.0)
    empty = (1.0 - jnp.sum(place, axis=1, keepdims=True)) * EMPTY
    place = place.astype(jnp.bfloat16)

    for i in (0, 1, 2):
        loads[i].wait()
    projected = (dot(tokens[...], proj[...]) - mean[...].reshape(1, -1)).astype(jnp.bfloat16)
    for i in (5, 6):
        loads[i].start()
    loads[4].wait()
    pl.semaphore_wait(barrier, SPANS - 1 + 4)

    a2a = []
    for c, (lo, hi) in enumerate(chunks):
        t_send, t_recv = buf[c][0], buf[c][1]
        target = dot_t(projected, rotate[lo:hi, :]).astype(jnp.bfloat16)
        t_send[...] = (dot(place, target) + empty).astype(jnp.bfloat16)
        for step in (2, 3, 1):
            other = lax.rem(span + step, SPANS)
            copy = pltpu.make_async_remote_copy(
                src_ref=t_send.at[pl.ds(pl.multiple_of(other * cap, 16), cap)],
                dst_ref=t_recv.at[pl.ds(pl.multiple_of(span * cap, 16), cap)],
                send_sem=a2a_send.at[c, step - 1],
                recv_sem=a2a_recv.at[c, step - 1],
                device_id=(other, me),
                device_id_type=MESH,
            )
            copy.start()
            a2a.append(copy)
        mine = pl.ds(pl.multiple_of(span * cap, 16), cap)
        t_recv[mine, :] = t_send[mine, :]

    loads[5].wait()
    for j in range(0, width, 128):
        x = hidden[:, j : j + 128].astype(jnp.float32)
        a = (0.5 * x * (1.0 + lax.erf(x * (0.5**0.5)))).astype(jnp.bfloat16)
        act[:, j : j + 128] = a
        a_t = a.T
        at = j
        while at < j + 128:
            index = at // block
            end = min(j + 128, (index + 1) * block)
            own_core = core if index % 2 == 1 else 1 - core
            to = own_core * group + index // 2 * block + at % block
            act_t[pl.ds(pl.multiple_of(to, 16), end - at), :] = a_t[at - j : end - j, :]
            at = end
    loads[6].wait()
    pred[...] = dot_t(act[...], adaptor[...])

    sends = []

    def send(src, dst, send_sem, recv_sem, device):
        copy = pltpu.make_async_remote_copy(
            src_ref=src,
            dst_ref=dst,
            send_sem=send_sem,
            recv_sem=recv_sem,
            device_id=device,
            device_id_type=MESH,
        )
        copy.start()
        return copy

    class Pair:
        def __init__(self, c, src, dst, sems, device):
            self.copies = [
                pltpu.make_async_remote_copy(
                    src_ref=buf[c][src + 6 * i],
                    dst_ref=buf[c][dst + 6 * i],
                    send_sem=sems[i],
                    recv_sem=sems[2 + i],
                    device_id=device,
                    device_id_type=MESH,
                )
                for i in range(2)
            ]

        def start(self):
            for copy in self.copies:
                copy.start()

        def wait_recv(self):
            for copy in self.copies:
                copy.wait_recv()

        def wait_send(self):
            for copy in self.copies:
                copy.wait_send()

    def put(values, c, at):
        encode(values, buf[c][at], buf[c][at + 6])

    def get(c, at):
        return decode(buf[c][at], buf[c][at + 6])

    core_copies = {}
    plane_copies = {}
    z_copies = {}

    def rows_of(index):
        return pl.ds(pl.multiple_of(index * block, 16), block)

    def form(c):
        lo, hi = chunks[c]
        t_recv, core_out, core_in, total = buf[c][1], buf[c][2], buf[c][3], buf[c][4]
        for copy in a2a[3 * c : 3 * c + 3]:
            copy.wait_recv()
        t = t_recv[...].astype(jnp.float32)
        error = jnp.where(t > EMPTY_TEST, 0.0, (pred[:, lo:hi] - t) * (1.0 / features)).astype(
            jnp.bfloat16
        )
        core_out[...] = dot(act_t[:group, :], error).astype(jnp.bfloat16)
        core_copies[c] = send(
            core_out, core_in, core_sem.at[c, 0], core_sem.at[c, 1], (span, core_mate)
        )
        total[...] = dot(act_t[group:, :], error)

    def plane(c):
        core_in, total, plane_out, plane_in = buf[c][3], buf[c][4], buf[c][5], buf[c][6]
        core_copies[c].wait_recv()
        for j, mate in enumerate(plane_mates):
            away = rows_of(mate // 2)
            plane_out[j] = (total[away, :] + core_in[away, :]).astype(jnp.bfloat16)
            plane_copies[c, j] = send(
                plane_out.at[j],
                plane_in.at[j],
                plane_send.at[c, j],
                plane_recv.at[c, j],
                (span, mate),
            )

    def z_send(c, stage):
        at = 7 + 2 * stage
        z_copies[c, stage] = Pair(
            c, at, at + 1, [z_sem.at[c, stage, i] for i in range(4)], (z_mates[stage % 2], me)
        )
        z_copies[c, stage].start()

    odd = lax.rem(span, 2)
    kept_half = pl.ds(pl.multiple_of(odd * half, 16), half)
    given_half = pl.ds(pl.multiple_of((1 - odd) * half, 16), half)

    def first_z(c):
        core_in, total, plane_in, own = buf[c][3], buf[c][4], buf[c][6], buf[c][19]
        here = rows_of(me // 2)
        value = total[here, :] + core_in[here, :]
        for j in range(3):
            plane_copies[c, j].wait_recv()
            value = value + plane_in[j]
        own[...] = value
        put(own[given_half, :], c, 7)
        z_send(c, 0)

    def second_z(c):
        z_copies[c, 0].wait_recv()
        put(buf[c][19][kept_half, :] + get(c, 8), c, 9)
        z_send(c, 1)

    def third_z(c):
        z_copies[c, 1].wait_recv()
        mine, other = get(c, 9), get(c, 10)
        low = jnp.where(span < 2, mine, other)
        high = jnp.where(span < 2, other, mine)
        put(low + high, c, 11)
        z_send(c, 2)

    def finish(c):
        lo, hi = chunks[c]
        z_copies[c, 2].wait_recv()
        out[kept_half, lo:hi] = get(c, 11)
        out[given_half, lo:hi] = get(c, 12)

    n = len(chunks)
    for c in range(n):
        form(c)
        if c >= 1:
            first_z(c - 1)
        if c >= 2:
            second_z(c - 2)
        plane(c)
        if c >= 3:
            third_z(c - 3)
        if c >= 4:
            finish(c - 4)
    for c in range(n, n + 4):
        for stage, step in ((2, second_z), (1, first_z), (3, third_z), (4, finish)):
            if 0 <= c - stage < n:
                step(c - stage)

    for copy in a2a:
        copy.wait_send()
    for group in (core_copies, plane_copies, z_copies):
        for copy in group.values():
            copy.wait_send()


def kernel_body(
    tokens,
    out_proj,
    phi_mean,
    phi_rotate,
    destinations,
    student_hidden,
    adaptor,
    master,
    moment_one,
    moment_two,
):
    rows = tokens.shape[0]
    slots, width = student_hidden.shape
    features = adaptor.shape[1]
    block = width // SHARDS
    chunks = chunks_of(features)
    bf16, f32 = jnp.bfloat16, jnp.float32
    dest = destinations.reshape(1, rows)
    inputs = (
        tokens,
        out_proj,
        phi_mean,
        phi_rotate.T,
        dest,
        student_hidden,
        adaptor.T,
    )
    scratch = [pltpu.VMEM(a.shape, a.dtype) for a in inputs]
    scratch += [
        pltpu.VMEM((slots, width), bf16),
        pltpu.VMEM((width, slots), bf16),
        pltpu.VMEM((slots, features), f32),
    ]
    for lo, hi in chunks:
        wide = hi - lo
        scratch += [pltpu.VMEM((slots, wide), bf16)] * 2
        scratch += [pltpu.VMEM((width // 2, wide), bf16)] * 2
        scratch += [pltpu.VMEM((width // 2, wide), f32)]
        scratch += [pltpu.VMEM((3, block, wide), bf16)] * 2
        scratch += [pltpu.VMEM((block // 2, wide), jnp.int16)] * 6
        scratch += [pltpu.VMEM((8, 128), f32)] * 6
        scratch += [pltpu.VMEM((block, wide), f32)]
    n = len(chunks)
    dma = pltpu.SemaphoreType.DMA
    scratch += [
        dma((len(inputs),)),
        dma((n, SPANS - 1)),
        dma((n, SPANS - 1)),
        dma((n, 2)),
        dma((n, 3)),
        dma((n, 3)),
        dma((n, 3, 4)),
    ]
    flops = 2 * (rows * tokens.shape[1] * (tokens.shape[1] + features) + 2 * slots * width * features)
    gradient = pl.pallas_call(
        functools.partial(step_kernel, chunks),
        out_shape=jax.ShapeDtypeStruct(master.shape, f32),
        in_specs=[pl.BlockSpec(memory_space=pl.ANY)] * len(inputs),
        out_specs=pl.BlockSpec(memory_space=pltpu.VMEM),
        scratch_shapes=scratch,
        compiler_params=pltpu.CompilerParams(
            collective_id=0, has_side_effects=True, vmem_limit_bytes=62 * 2**20
        ),
        cost_estimate=pl.CostEstimate(
            flops=flops, bytes_accessed=10 * 2**20, transcendentals=slots * width
        ),
    )(*inputs)
    return adam_update(gradient, master, moment_one, moment_two)


def solution(mesh):
    in_specs = (
        P(("span", "shard"), None),
        P(),
        P(),
        P(),
        P(("span", "shard"), None),
        P(("span", "shard"), None),
        P(),
        P("shard", None),
        P("shard", None),
        P("shard", None),
    )
    out_specs = (P("shard", None), P("shard", None), P("shard", None))
    tuned = mesh.shape["span"] == SPANS and mesh.shape["shard"] == SHARDS
    body = kernel_body if tuned else general_body
    return jax.shard_map(body, mesh=mesh, in_specs=in_specs, out_specs=out_specs, check_vma=False)
```

```python
import functools

import jax
import jax.numpy as jnp
from jax import lax
from jax.experimental import pallas as pl
from jax.experimental.pallas import tpu as pltpu
from jax.sharding import PartitionSpec as P

ADAM_STEP = 1000


beta_first = 0.9
beta_second = 0.999
adam_epsilon = 1e-08
decay_rate = 0.05
learn_rate = 0.001

EMPTY = 2.0**100
EMPTY_TEST = 2.0**90
MESH = pl.DeviceIdType.MESH


def adam_update(gradient, master, moment_one, moment_two):
    first_new = beta_first * moment_one + (1.0 - beta_first) * gradient
    second_new = beta_second * moment_two + (1.0 - beta_second) * gradient * gradient
    bias_first = 1.0 - beta_first**ADAM_STEP
    bias_second = 1.0 - beta_second**ADAM_STEP
    update_dir = (
        first_new / bias_first / (jnp.sqrt(second_new / bias_second) + adam_epsilon)
        + decay_rate * master
    )
    return (master - learn_rate * update_dir, first_new, second_new)


def route_slots(destinations, span_count, capacity):
    target_span = destinations[:, 0]
    span_ids = jnp.arange(span_count, dtype=jnp.int32)
    one_hot = (target_span[:, None] == span_ids[None, :]).astype(jnp.int32)
    before = jnp.cumsum(one_hot, axis=0) - one_hot
    slot_rank = jnp.sum(before * one_hot, axis=1)
    return target_span * capacity + slot_rank


def general_body(
    tokens,
    out_proj,
    phi_mean,
    phi_rotate,
    destinations,
    student_hidden,
    adaptor,
    master,
    moment_one,
    moment_two,
):
    span_count = lax.axis_size("span")
    slots = student_hidden.shape[0]
    capacity = slots // span_count
    features = adaptor.shape[1]
    projected = (jnp.dot(tokens, out_proj, preferred_element_type=jnp.float32) - phi_mean).astype(
        jnp.bfloat16
    )
    target = jnp.dot(projected, phi_rotate, preferred_element_type=jnp.float32).astype(jnp.bfloat16)
    slot_ids = route_slots(destinations, span_count, capacity)
    placed = jnp.full((slots, features), EMPTY, jnp.bfloat16).at[slot_ids].set(target)
    arrived = lax.all_to_all(
        placed.reshape(span_count, capacity, features), "span", split_axis=0, concat_axis=0, tiled=True
    ).reshape(slots, features)
    activated = jax.nn.gelu(student_hidden.astype(jnp.float32), approximate=False).astype(jnp.bfloat16)
    predicted = jnp.dot(activated, adaptor, preferred_element_type=jnp.float32)
    wanted = arrived.astype(jnp.float32)
    scaled_error = jnp.where(wanted > EMPTY_TEST, 0.0, (predicted - wanted) / features).astype(
        jnp.bfloat16
    )
    contract = (((0,), (0,)), ((), ()))
    partial_sum = lax.psum_scatter(
        lax.dot_general(activated, scaled_error, contract, preferred_element_type=jnp.float32),
        "shard",
        scatter_dimension=0,
        tiled=True,
    )
    return adam_update(lax.psum(partial_sum, "span"), master, moment_one, moment_two)


SPANS = 4
SHARDS = 8


def chunks_of(features):
    return tuple((lo, min(lo + 128, features)) for lo in range(0, features, 128))


def dot(a, b):
    return jnp.dot(a, b, preferred_element_type=jnp.float32)


def dot_t(a, b):
    return lax.dot_general(a, b, (((1,), (1,)), ((), ())), preferred_element_type=jnp.float32)


def encode(values, codes, scale):
    top = jnp.max(jnp.max(jnp.abs(values), axis=0, keepdims=True), axis=1, keepdims=True)
    top = jnp.maximum(top, 1e-30)
    codes[...] = jnp.round(values * (32000.0 / top)).astype(jnp.int32).astype(jnp.int16)
    scale[...] = jnp.broadcast_to(top * (1.0 / 32000.0), scale.shape)


def decode(codes, scale):
    return codes[...].astype(jnp.int32).astype(jnp.float32) * scale[0:1, 0:1]


def step_kernel(
    chunks,
    tokens_hbm,
    proj_hbm,
    mean_hbm,
    rotate_hbm,
    dest_hbm,
    hidden_hbm,
    adaptor_hbm,
    out,
    tokens,
    proj,
    mean,
    rotate,
    dest,
    hidden,
    adaptor,
    act,
    act_t,
    pred,
    *rest,
):
    per_chunk, (load_sem, a2a_send, a2a_recv, core_sem, plane_send, plane_recv, z_sem) = (
        rest[:-7],
        rest[-7:],
    )
    count = len(per_chunk) // len(chunks)
    buf = [per_chunk[c * count : (c + 1) * count] for c in range(len(chunks))]

    span = lax.axis_index("span")
    me = lax.axis_index("shard")
    core = lax.rem(me, 2)
    my_x = lax.rem(me // 2, 2)
    my_y = me // 4
    core_mate = me + 1 - 2 * core
    x_mate = me + 2 - 4 * my_x
    y_mate = me + 4 - 8 * my_y
    cross_mate = y_mate + 2 - 4 * my_x
    plane_mates = (x_mate, y_mate, cross_mate)
    z_mates = (span + 1 - 2 * lax.rem(span, 2), span + 2 - 4 * (span // 2))

    slots, width = hidden.shape
    rows = tokens.shape[0]
    features = adaptor.shape[0]
    cap = slots // SPANS
    block = width // SHARDS
    group = width // 2

    pairs = (
        (tokens_hbm, tokens),
        (proj_hbm, proj),
        (mean_hbm, mean),
        (dest_hbm, dest),
        (rotate_hbm, rotate),
        (hidden_hbm, hidden),
        (adaptor_hbm, adaptor),
    )
    loads = [pltpu.make_async_copy(s, d, load_sem.at[i]) for i, (s, d) in enumerate(pairs)]
    for i in (0, 1, 2, 3, 4):
        loads[i].start()

    barrier = pltpu.get_barrier_semaphore()
    for step in range(1, SPANS):
        pl.semaphore_signal(
            barrier, inc=1, device_id=(lax.rem(span + step, SPANS), me), device_id_type=MESH
        )
    for mate in (core_mate, *plane_mates):
        pl.semaphore_signal(barrier, inc=1, device_id=(span, mate), device_id_type=MESH)

    loads[3].wait()
    wanted = dest[...]
    span_ids = lax.broadcasted_iota(jnp.int32, (16, rows), 0)
    one_hot = jnp.where(span_ids == wanted, 1.0, 0.0)
    earlier = jnp.where(
        lax.broadcasted_iota(jnp.int32, (rows, rows), 0)
        < lax.broadcasted_iota(jnp.int32, (rows, rows), 1),
        1.0,
        0.0,
    ).astype(jnp.bfloat16)
    before = dot(one_hot.astype(jnp.bfloat16), earlier)
    rank = jnp.sum(before * one_hot, axis=0, keepdims=True).astype(jnp.int32)
    slot = wanted * cap + rank
    place = jnp.where(lax.broadcasted_iota(jnp.int32, (slots, rows), 0) == slot, 1.0, 0.0)
    empty = (1.0 - jnp.sum(place, axis=1, keepdims=True)) * EMPTY
    place = place.astype(jnp.bfloat16)

    for i in (0, 1, 2):
        loads[i].wait()
    projected = (dot(tokens[...], proj[...]) - mean[...].reshape(1, -1)).astype(jnp.bfloat16)
    for i in (5, 6):
        loads[i].start()
    loads[4].wait()
    pl.semaphore_wait(barrier, SPANS - 1 + 4)

    a2a = []
    for c, (lo, hi) in enumerate(chunks):
        t_send, t_recv = buf[c][0], buf[c][1]
        target = dot_t(projected, rotate[lo:hi, :]).astype(jnp.bfloat16)
        t_send[...] = (dot(place, target) + empty).astype(jnp.bfloat16)
        for step in (2, 3, 1):
            other = lax.rem(span + step, SPANS)
            copy = pltpu.make_async_remote_copy(
                src_ref=t_send.at[pl.ds(pl.multiple_of(other * cap, 16), cap)],
                dst_ref=t_recv.at[pl.ds(pl.multiple_of(span * cap, 16), cap)],
                send_sem=a2a_send.at[c, step - 1],
                recv_sem=a2a_recv.at[c, step - 1],
                device_id=(other, me),
                device_id_type=MESH,
            )
            copy.start()
            a2a.append(copy)
        mine = pl.ds(pl.multiple_of(span * cap, 16), cap)
        t_recv[mine, :] = t_send[mine, :]

    loads[5].wait()
    for j in range(0, width, 128):
        x = hidden[:, j : j + 128].astype(jnp.float32)
        a = (0.5 * x * (1.0 + lax.erf(x * (0.5**0.5)))).astype(jnp.bfloat16)
        act[:, j : j + 128] = a
        a_t = a.T
        at = j
        while at < j + 128:
            index = at // block
            end = min(j + 128, (index + 1) * block)
            own_core = core if index % 2 == 1 else 1 - core
            to = own_core * group + index // 2 * block + at % block
            act_t[pl.ds(pl.multiple_of(to, 16), end - at), :] = a_t[at - j : end - j, :]
            at = end
    loads[6].wait()
    pred[...] = dot_t(act[...], adaptor[...])

    sends = []

    def send(src, dst, send_sem, recv_sem, device):
        copy = pltpu.make_async_remote_copy(
            src_ref=src,
            dst_ref=dst,
            send_sem=send_sem,
            recv_sem=recv_sem,
            device_id=device,
            device_id_type=MESH,
        )
        copy.start()
        return copy

    class Pair:
        def __init__(self, sources, targets, sems, device):
            self.copies = [
                pltpu.make_async_remote_copy(
                    src_ref=sources[i],
                    dst_ref=targets[i],
                    send_sem=sems[i],
                    recv_sem=sems[2 + i],
                    device_id=device,
                    device_id_type=MESH,
                )
                for i in range(2)
            ]

        def start(self):
            for copy in self.copies:
                copy.start()

        def wait_recv(self):
            for copy in self.copies:
                copy.wait_recv()

        def wait_send(self):
            for copy in self.copies:
                copy.wait_send()

    core_copies = {}
    plane_copies = {}
    z_copies = {}

    def rows_of(index):
        return pl.ds(pl.multiple_of(index * block, 16), block)

    def form(c):
        lo, hi = chunks[c]
        t_recv, core_out, core_in, total = buf[c][1], buf[c][2], buf[c][3], buf[c][4]
        for copy in a2a[3 * c : 3 * c + 3]:
            copy.wait_recv()
        t = t_recv[...].astype(jnp.float32)
        error = jnp.where(t > EMPTY_TEST, 0.0, (pred[:, lo:hi] - t) * (1.0 / features)).astype(
            jnp.bfloat16
        )
        core_out[...] = dot(act_t[:group, :], error).astype(jnp.bfloat16)
        core_copies[c] = send(
            core_out, core_in, core_sem.at[c, 0], core_sem.at[c, 1], (span, core_mate)
        )
        total[...] = dot(act_t[group:, :], error)

    def plane(c):
        core_in, total, plane_out, plane_in = buf[c][3], buf[c][4], buf[c][5], buf[c][6]
        core_copies[c].wait_recv()
        for j, mate in enumerate(plane_mates):
            away = rows_of(mate // 2)
            plane_out[j] = (total[away, :] + core_in[away, :]).astype(jnp.bfloat16)
            plane_copies[c, j] = send(
                plane_out.at[j],
                plane_in.at[j],
                plane_send.at[c, j],
                plane_recv.at[c, j],
                (span, mate),
            )

    n = len(chunks)
    z_low = (lax.rem(span, 2) == 0, span < 2)

    def parts(c, at):
        return buf[c][7].at[at], buf[c][8].at[at]

    def z_send(c, stage, source, target, device):
        z_copies[c, stage] = Pair(
            parts(c, source),
            parts(c, target),
            [z_sem.at[c, stage, i] for i in range(4)],
            (device, me),
        )
        z_copies[c, stage].start()

    def at_once(c):
        return c >= n - 2

    def z_sum(c, stage):
        z_copies[c, stage].wait_recv()
        mine, other = decode(*parts(c, 2 * stage)), decode(*parts(c, 2 * stage + 1))
        low = jnp.where(z_low[stage], mine, other)
        high = jnp.where(z_low[stage], other, mine)
        return low + high

    def first_z(c):
        core_in, total, plane_in = buf[c][3], buf[c][4], buf[c][6]
        here = rows_of(me // 2)
        value = total[here, :] + core_in[here, :]
        for j in range(3):
            plane_copies[c, j].wait_recv()
            value = value + plane_in[j]
        if at_once(c):
            encode(value, *parts(c, span))
            for j, step in enumerate((2, 3, 1)):
                z_send(c, j, span, span, lax.rem(span + step, SPANS))
        else:
            encode(value, *parts(c, 0))
            z_send(c, 0, 0, 1, z_mates[0])

    def second_z(c):
        if not at_once(c):
            encode(z_sum(c, 0), *parts(c, 2))
            z_send(c, 1, 2, 3, z_mates[1])

    def finish(c):
        lo, hi = chunks[c]
        if at_once(c):
            for j in range(3):
                z_copies[c, j].wait_recv()
            sum_z = decode(*parts(c, 0))
            for j in range(1, SPANS):
                sum_z = sum_z + decode(*parts(c, j))
        else:
            sum_z = z_sum(c, 1)
        out[:, lo:hi] = sum_z

    for c in range(n):
        form(c)
        if c >= 1:
            first_z(c - 1)
        if c >= 2:
            second_z(c - 2)
        plane(c)
        if c >= 3:
            finish(c - 3)
    first_z(n - 1)
    for c in range(n - 3, n):
        finish(c)

    for copy in a2a:
        copy.wait_send()
    for group in (core_copies, plane_copies, z_copies):
        for copy in group.values():
            copy.wait_send()


def kernel_body(
    tokens,
    out_proj,
    phi_mean,
    phi_rotate,
    destinations,
    student_hidden,
    adaptor,
    master,
    moment_one,
    moment_two,
):
    rows = tokens.shape[0]
    slots, width = student_hidden.shape
    features = adaptor.shape[1]
    block = width // SHARDS
    chunks = chunks_of(features)
    bf16, f32 = jnp.bfloat16, jnp.float32
    dest = destinations.reshape(1, rows)
    inputs = (
        tokens,
        out_proj,
        phi_mean,
        phi_rotate.T,
        dest,
        student_hidden,
        adaptor.T,
    )
    scratch = [pltpu.VMEM(a.shape, a.dtype) for a in inputs]
    scratch += [
        pltpu.VMEM((slots, width), bf16),
        pltpu.VMEM((width, slots), bf16),
        pltpu.VMEM((slots, features), f32),
    ]
    for lo, hi in chunks:
        wide = hi - lo
        scratch += [pltpu.VMEM((slots, wide), bf16)] * 2
        scratch += [pltpu.VMEM((width // 2, wide), bf16)] * 2
        scratch += [pltpu.VMEM((width // 2, wide), f32)]
        scratch += [pltpu.VMEM((3, block, wide), bf16)] * 2
        scratch += [pltpu.VMEM((SPANS, block, wide), jnp.int16)]
        scratch += [pltpu.VMEM((SPANS, 8, 128), f32)]
    n = len(chunks)
    dma = pltpu.SemaphoreType.DMA
    scratch += [
        dma((len(inputs),)),
        dma((n, SPANS - 1)),
        dma((n, SPANS - 1)),
        dma((n, 2)),
        dma((n, 3)),
        dma((n, 3)),
        dma((n, 3, 4)),
    ]
    flops = 2 * (rows * tokens.shape[1] * (tokens.shape[1] + features) + 2 * slots * width * features)
    gradient = pl.pallas_call(
        functools.partial(step_kernel, chunks),
        out_shape=jax.ShapeDtypeStruct(master.shape, f32),
        in_specs=[pl.BlockSpec(memory_space=pl.ANY)] * len(inputs),
        out_specs=pl.BlockSpec(memory_space=pltpu.VMEM),
        scratch_shapes=scratch,
        compiler_params=pltpu.CompilerParams(
            collective_id=0, has_side_effects=True, vmem_limit_bytes=62 * 2**20
        ),
        cost_estimate=pl.CostEstimate(
            flops=flops, bytes_accessed=10 * 2**20, transcendentals=slots * width
        ),
    )(*inputs)
    return adam_update(gradient, master, moment_one, moment_two)


def solution(mesh):
    in_specs = (
        P(("span", "shard"), None),
        P(),
        P(),
        P(),
        P(("span", "shard"), None),
        P(("span", "shard"), None),
        P(),
        P("shard", None),
        P("shard", None),
        P("shard", None),
    )
    out_specs = (P("shard", None), P("shard", None), P("shard", None))
    tuned = mesh.shape["span"] == SPANS and mesh.shape["shard"] == SHARDS
    body = kernel_body if tuned else general_body
    return jax.shard_map(body, mesh=mesh, in_specs=in_specs, out_specs=out_specs, check_vma=False)
```

```python
import functools

import jax
import jax.numpy as jnp
from jax import lax
from jax.experimental import pallas as pl
from jax.experimental.pallas import tpu as pltpu
from jax.sharding import PartitionSpec as P

ADAM_STEP = 1000


beta_first = 0.9
beta_second = 0.999
adam_epsilon = 1e-08
decay_rate = 0.05
learn_rate = 0.001

EMPTY = 2.0**100
EMPTY_TEST = 2.0**90
MESH = pl.DeviceIdType.MESH


def adam_update(gradient, master, moment_one, moment_two):
    first_new = beta_first * moment_one + (1.0 - beta_first) * gradient
    second_new = beta_second * moment_two + (1.0 - beta_second) * gradient * gradient
    bias_first = 1.0 - beta_first**ADAM_STEP
    bias_second = 1.0 - beta_second**ADAM_STEP
    update_dir = (
        first_new / bias_first / (jnp.sqrt(second_new / bias_second) + adam_epsilon)
        + decay_rate * master
    )
    return (master - learn_rate * update_dir, first_new, second_new)


def route_slots(destinations, span_count, capacity):
    target_span = destinations[:, 0]
    span_ids = jnp.arange(span_count, dtype=jnp.int32)
    one_hot = (target_span[:, None] == span_ids[None, :]).astype(jnp.int32)
    before = jnp.cumsum(one_hot, axis=0) - one_hot
    slot_rank = jnp.sum(before * one_hot, axis=1)
    return target_span * capacity + slot_rank


def general_body(
    tokens,
    out_proj,
    phi_mean,
    phi_rotate,
    destinations,
    student_hidden,
    adaptor,
    master,
    moment_one,
    moment_two,
):
    span_count = lax.axis_size("span")
    slots = student_hidden.shape[0]
    capacity = slots // span_count
    features = adaptor.shape[1]
    projected = (jnp.dot(tokens, out_proj, preferred_element_type=jnp.float32) - phi_mean).astype(
        jnp.bfloat16
    )
    target = jnp.dot(projected, phi_rotate, preferred_element_type=jnp.float32).astype(jnp.bfloat16)
    slot_ids = route_slots(destinations, span_count, capacity)
    placed = jnp.full((slots, features), EMPTY, jnp.bfloat16).at[slot_ids].set(target)
    arrived = lax.all_to_all(
        placed.reshape(span_count, capacity, features), "span", split_axis=0, concat_axis=0, tiled=True
    ).reshape(slots, features)
    activated = jax.nn.gelu(student_hidden.astype(jnp.float32), approximate=False).astype(jnp.bfloat16)
    predicted = jnp.dot(activated, adaptor, preferred_element_type=jnp.float32)
    wanted = arrived.astype(jnp.float32)
    scaled_error = jnp.where(wanted > EMPTY_TEST, 0.0, (predicted - wanted) / features).astype(
        jnp.bfloat16
    )
    contract = (((0,), (0,)), ((), ()))
    partial_sum = lax.psum_scatter(
        lax.dot_general(activated, scaled_error, contract, preferred_element_type=jnp.float32),
        "shard",
        scatter_dimension=0,
        tiled=True,
    )
    return adam_update(lax.psum(partial_sum, "span"), master, moment_one, moment_two)


SPANS = 4
SHARDS = 8


def chunks_of(features):
    return ((0, 256),) + tuple((lo, min(lo + 128, features)) for lo in range(256, features, 128))


def dot(a, b):
    return jnp.dot(a, b, preferred_element_type=jnp.float32)


def dot_t(a, b):
    return lax.dot_general(a, b, (((1,), (1,)), ((), ())), preferred_element_type=jnp.float32)


def encode(values, codes, scale):
    top = jnp.max(jnp.max(jnp.abs(values), axis=0, keepdims=True), axis=1, keepdims=True)
    top = jnp.maximum(top, 1e-30)
    codes[...] = jnp.round(values * (32000.0 / top)).astype(jnp.int32).astype(jnp.int16)
    scale[...] = jnp.broadcast_to(top * (1.0 / 32000.0), scale.shape)


def decode(codes, scale):
    return codes[...].astype(jnp.int32).astype(jnp.float32) * scale[0:1, 0:1]


def step_kernel(
    chunks,
    tokens_hbm,
    proj_hbm,
    mean_hbm,
    rotate_hbm,
    dest_hbm,
    hidden_hbm,
    adaptor_hbm,
    out,
    tokens,
    proj,
    mean,
    rotate,
    dest,
    hidden,
    adaptor,
    act,
    act_t,
    pred,
    *rest,
):
    per_chunk, (load_sem, a2a_send, a2a_recv, core_sem, plane_send, plane_recv, z_sem) = (
        rest[:-7],
        rest[-7:],
    )
    count = len(per_chunk) // len(chunks)
    buf = [per_chunk[c * count : (c + 1) * count] for c in range(len(chunks))]

    span = lax.axis_index("span")
    me = lax.axis_index("shard")
    core = lax.rem(me, 2)
    my_x = lax.rem(me // 2, 2)
    my_y = me // 4
    core_mate = me + 1 - 2 * core
    x_mate = me + 2 - 4 * my_x
    y_mate = me + 4 - 8 * my_y
    cross_mate = y_mate + 2 - 4 * my_x
    plane_mates = (x_mate, y_mate, cross_mate)
    z_mates = (span + 1 - 2 * lax.rem(span, 2), span + 2 - 4 * (span // 2))

    slots, width = hidden.shape
    rows = tokens.shape[0]
    features = adaptor.shape[0]
    cap = slots // SPANS
    block = width // SHARDS
    group = width // 2

    pairs = (
        (tokens_hbm, tokens),
        (proj_hbm, proj),
        (mean_hbm, mean),
        (dest_hbm, dest),
        (rotate_hbm, rotate),
        (hidden_hbm, hidden),
        (adaptor_hbm, adaptor),
    )
    loads = [pltpu.make_async_copy(s, d, load_sem.at[i]) for i, (s, d) in enumerate(pairs)]
    for i in (0, 1, 2, 3, 4):
        loads[i].start()

    barrier = pltpu.get_barrier_semaphore()
    for step in range(1, SPANS):
        pl.semaphore_signal(
            barrier, inc=1, device_id=(lax.rem(span + step, SPANS), me), device_id_type=MESH
        )
    for mate in (core_mate, *plane_mates):
        pl.semaphore_signal(barrier, inc=1, device_id=(span, mate), device_id_type=MESH)

    loads[3].wait()
    wanted = dest[...]
    span_ids = lax.broadcasted_iota(jnp.int32, (16, rows), 0)
    one_hot = jnp.where(span_ids == wanted, 1.0, 0.0)
    earlier = jnp.where(
        lax.broadcasted_iota(jnp.int32, (rows, rows), 0)
        < lax.broadcasted_iota(jnp.int32, (rows, rows), 1),
        1.0,
        0.0,
    ).astype(jnp.bfloat16)
    before = dot(one_hot.astype(jnp.bfloat16), earlier)
    rank = jnp.sum(before * one_hot, axis=0, keepdims=True).astype(jnp.int32)
    slot = wanted * cap + rank
    place = jnp.where(lax.broadcasted_iota(jnp.int32, (slots, rows), 0) == slot, 1.0, 0.0)
    empty = (1.0 - jnp.sum(place, axis=1, keepdims=True)) * EMPTY
    place = place.astype(jnp.bfloat16)

    for i in (0, 1, 2):
        loads[i].wait()
    projected = (dot(tokens[...], proj[...]) - mean[...].reshape(1, -1)).astype(jnp.bfloat16)
    for i in (5, 6):
        loads[i].start()
    loads[4].wait()
    pl.semaphore_wait(barrier, SPANS - 1 + 4)

    a2a = []
    for c, (lo, hi) in enumerate(chunks):
        t_send, t_recv = buf[c][0], buf[c][1]
        target = dot_t(projected, rotate[lo:hi, :]).astype(jnp.bfloat16)
        t_send[...] = (dot(place, target) + empty).astype(jnp.bfloat16)
        for step in (2, 3, 1):
            other = lax.rem(span + step, SPANS)
            copy = pltpu.make_async_remote_copy(
                src_ref=t_send.at[pl.ds(pl.multiple_of(other * cap, 16), cap)],
                dst_ref=t_recv.at[pl.ds(pl.multiple_of(span * cap, 16), cap)],
                send_sem=a2a_send.at[c, step - 1],
                recv_sem=a2a_recv.at[c, step - 1],
                device_id=(other, me),
                device_id_type=MESH,
            )
            copy.start()
            a2a.append(copy)
        mine = pl.ds(pl.multiple_of(span * cap, 16), cap)
        t_recv[mine, :] = t_send[mine, :]

    loads[5].wait()
    for j in range(0, width, 128):
        x = hidden[:, j : j + 128].astype(jnp.float32)
        a = (0.5 * x * (1.0 + lax.erf(x * (0.5**0.5)))).astype(jnp.bfloat16)
        act[:, j : j + 128] = a
        a_t = a.T
        at = j
        while at < j + 128:
            index = at // block
            end = min(j + 128, (index + 1) * block)
            own_core = core if index % 2 == 1 else 1 - core
            to = own_core * group + index // 2 * block + at % block
            act_t[pl.ds(pl.multiple_of(to, 16), end - at), :] = a_t[at - j : end - j, :]
            at = end
    loads[6].wait()
    pred[...] = dot_t(act[...], adaptor[...])

    sends = []

    def send(src, dst, send_sem, recv_sem, device):
        copy = pltpu.make_async_remote_copy(
            src_ref=src,
            dst_ref=dst,
            send_sem=send_sem,
            recv_sem=recv_sem,
            device_id=device,
            device_id_type=MESH,
        )
        copy.start()
        return copy

    class Pair:
        def __init__(self, sources, targets, sems, device):
            self.copies = [
                pltpu.make_async_remote_copy(
                    src_ref=sources[i],
                    dst_ref=targets[i],
                    send_sem=sems[i],
                    recv_sem=sems[2 + i],
                    device_id=device,
                    device_id_type=MESH,
                )
                for i in range(2)
            ]

        def start(self):
            for copy in self.copies:
                copy.start()

        def wait_recv(self):
            for copy in self.copies:
                copy.wait_recv()

        def wait_send(self):
            for copy in self.copies:
                copy.wait_send()

    core_copies = {}
    plane_copies = {}
    z_copies = {}

    def rows_of(index):
        return pl.ds(pl.multiple_of(index * block, 16), block)

    def form(c):
        lo, hi = chunks[c]
        t_recv, core_out, core_in, total = buf[c][1], buf[c][2], buf[c][3], buf[c][4]
        for copy in a2a[3 * c : 3 * c + 3]:
            copy.wait_recv()
        t = t_recv[...].astype(jnp.float32)
        error = jnp.where(t > EMPTY_TEST, 0.0, (pred[:, lo:hi] - t) * (1.0 / features)).astype(
            jnp.bfloat16
        )
        core_out[...] = dot(act_t[:group, :], error).astype(jnp.bfloat16)
        core_copies[c] = send(
            core_out, core_in, core_sem.at[c, 0], core_sem.at[c, 1], (span, core_mate)
        )
        total[...] = dot(act_t[group:, :], error)

    def plane(c):
        core_in, total, plane_out, plane_in = buf[c][3], buf[c][4], buf[c][5], buf[c][6]
        core_copies[c].wait_recv()
        for j, mate in enumerate(plane_mates):
            away = rows_of(mate // 2)
            plane_out[j] = (total[away, :] + core_in[away, :]).astype(jnp.bfloat16)
            plane_copies[c, j] = send(
                plane_out.at[j],
                plane_in.at[j],
                plane_send.at[c, j],
                plane_recv.at[c, j],
                (span, mate),
            )

    n = len(chunks)
    z_low = (lax.rem(span, 2) == 0, span < 2)

    def parts(c, at):
        return buf[c][7].at[at], buf[c][8].at[at]

    def z_send(c, stage, source, target, device):
        z_copies[c, stage] = Pair(
            parts(c, source),
            parts(c, target),
            [z_sem.at[c, stage, i] for i in range(4)],
            (device, me),
        )
        z_copies[c, stage].start()

    def at_once(c):
        return c >= n - 2

    def z_sum(c, stage):
        z_copies[c, stage].wait_recv()
        mine, other = decode(*parts(c, 2 * stage)), decode(*parts(c, 2 * stage + 1))
        low = jnp.where(z_low[stage], mine, other)
        high = jnp.where(z_low[stage], other, mine)
        return low + high

    def first_z(c):
        core_in, total, plane_in = buf[c][3], buf[c][4], buf[c][6]
        here = rows_of(me // 2)
        value = total[here, :] + core_in[here, :]
        for j in range(3):
            plane_copies[c, j].wait_recv()
            value = value + plane_in[j]
        if at_once(c):
            encode(value, *parts(c, span))
            for j, step in enumerate((2, 3, 1)):
                z_send(c, j, span, span, lax.rem(span + step, SPANS))
        else:
            encode(value, *parts(c, 0))
            z_send(c, 0, 0, 1, z_mates[0])

    def second_z(c):
        if not at_once(c):
            encode(z_sum(c, 0), *parts(c, 2))
            z_send(c, 1, 2, 3, z_mates[1])

    def finish(c):
        lo, hi = chunks[c]
        if at_once(c):
            for j in range(3):
                z_copies[c, j].wait_recv()
            sum_z = decode(*parts(c, 0))
            for j in range(1, SPANS):
                sum_z = sum_z + decode(*parts(c, j))
        else:
            sum_z = z_sum(c, 1)
        out[:, lo:hi] = sum_z

    for c in range(n):
        form(c)
        if c >= 1:
            first_z(c - 1)
        if c >= 2:
            second_z(c - 2)
        plane(c)
        if c >= 3:
            finish(c - 3)
    first_z(n - 1)
    for c in range(n - 3, n):
        finish(c)

    for copy in a2a:
        copy.wait_send()
    for group in (core_copies, plane_copies, z_copies):
        for copy in group.values():
            copy.wait_send()


def kernel_body(
    tokens,
    out_proj,
    phi_mean,
    phi_rotate,
    destinations,
    student_hidden,
    adaptor,
    master,
    moment_one,
    moment_two,
):
    rows = tokens.shape[0]
    slots, width = student_hidden.shape
    features = adaptor.shape[1]
    block = width // SHARDS
    chunks = chunks_of(features)
    bf16, f32 = jnp.bfloat16, jnp.float32
    dest = destinations.reshape(1, rows)
    inputs = (
        tokens,
        out_proj,
        phi_mean,
        phi_rotate.T,
        dest,
        student_hidden,
        adaptor.T,
    )
    scratch = [pltpu.VMEM(a.shape, a.dtype) for a in inputs]
    scratch += [
        pltpu.VMEM((slots, width), bf16),
        pltpu.VMEM((width, slots), bf16),
        pltpu.VMEM((slots, features), f32),
    ]
    for lo, hi in chunks:
        wide = hi - lo
        scratch += [pltpu.VMEM((slots, wide), bf16)] * 2
        scratch += [pltpu.VMEM((width // 2, wide), bf16)] * 2
        scratch += [pltpu.VMEM((width // 2, wide), f32)]
        scratch += [pltpu.VMEM((3, block, wide), bf16)] * 2
        scratch += [pltpu.VMEM((SPANS, block, wide), jnp.int16)]
        scratch += [pltpu.VMEM((SPANS, 8, 128), f32)]
    n = len(chunks)
    dma = pltpu.SemaphoreType.DMA
    scratch += [
        dma((len(inputs),)),
        dma((n, SPANS - 1)),
        dma((n, SPANS - 1)),
        dma((n, 2)),
        dma((n, 3)),
        dma((n, 3)),
        dma((n, 3, 4)),
    ]
    flops = 2 * (rows * tokens.shape[1] * (tokens.shape[1] + features) + 2 * slots * width * features)
    gradient = pl.pallas_call(
        functools.partial(step_kernel, chunks),
        out_shape=jax.ShapeDtypeStruct(master.shape, f32),
        in_specs=[pl.BlockSpec(memory_space=pl.ANY)] * len(inputs),
        out_specs=pl.BlockSpec(memory_space=pltpu.VMEM),
        scratch_shapes=scratch,
        compiler_params=pltpu.CompilerParams(
            collective_id=0, has_side_effects=True, vmem_limit_bytes=62 * 2**20
        ),
        cost_estimate=pl.CostEstimate(
            flops=flops, bytes_accessed=10 * 2**20, transcendentals=slots * width
        ),
    )(*inputs)
    return adam_update(gradient, master, moment_one, moment_two)


def solution(mesh):
    in_specs = (
        P(("span", "shard"), None),
        P(),
        P(),
        P(),
        P(("span", "shard"), None),
        P(("span", "shard"), None),
        P(),
        P("shard", None),
        P("shard", None),
        P("shard", None),
    )
    out_specs = (P("shard", None), P("shard", None), P("shard", None))
    tuned = mesh.shape["span"] == SPANS and mesh.shape["shard"] == SHARDS
    body = kernel_body if tuned else general_body
    return jax.shard_map(body, mesh=mesh, in_specs=in_specs, out_specs=out_specs, check_vma=False)
```
